32 devices in a mesh: groups: 2 (over x), tensor: 4 (over y, core), dp: 4 (over z).
Axes of the slice: x: 2, y: 2, z: 4, core: 2. Of those that a mesh axis runs over, the one named last changes fastest.
Arguments:
- queries: bfloat16 [4096, 12288], P(('groups', 'dp'), 'tensor'), parts along dimension 0, may hold values from -24 to 24
- keys: bfloat16 [4096, 1024], P(('groups', 'dp')), parts along dimension 0, may hold values from -14 to 14
- values: bfloat16 [4096, 1024], P(('groups', 'dp')), parts along dimension 0, may hold values from -6 to 6
- page_start: int32 [4096], P(('groups', 'dp')), parts along dimension 0, may hold values from 0 to 2047, as said below
Outputs:
- gram_band: float32 [24576, 9216], P(('groups', 'tensor', 'dp')), parts along dimension 0
The draws below stay inside these ranges and needn't reach their ends.
There are 2 independent parts, one for each index of `groups`. The reference program is written for one: setup_inputs(seed, part) draws one part's arguments, and reference() takes and returns one part's arrays. A program takes and returns all parts, laid end to end along the dimension named above; each array names one. Nothing has to cross between parts.
Inputs may be any that keep to these rules, and one draw needn't show every extreme that they name: p - page_start[p] < 512, page_start never falls and starts each page at its first position; some page has exactly 512 tokens, and pages cross from one run of 512 tokens into the next.
All inputs are finite; a program needn't handle non-finite values.
Results may differ from the reference program's by a relative error of at most 0.012.
Values may be sent and summed in bfloat16 or wider, within the bound.
No kernel may reach another device: no remote copies, remote signals or barrier semaphores. Data moves between devices by JAX's collectives and lax.ppermute only.
A program may use at most 256 MiB of HBM per device.

```python
import jax
import jax.numpy as jnp
from jax import lax

HEADS = 96
HD = 128
KV_HEADS = 8
PAGE = 512
TOK_DEV = 512
TOKENS = 2048
N_TENSOR = 4
N_DP = 4


def common_base(key):
    return jnp.clip(jax.random.normal(key, (TOKENS, KV_HEADS * HD), jnp.float32), -4.0, 4.0)


def draw_keys(key, part):
    base = common_base(key)
    result = base
    return result.astype(jnp.bfloat16)


def draw_queries(key, part):
    key = jax.random.fold_in(key, 7)
    result = jnp.clip(jax.random.normal(key, (TOKENS, HEADS * HD), jnp.float32), -4.0, 4.0)
    return result.astype(jnp.bfloat16)


def draw_page_start(key, part):
    key = jax.random.fold_in(key, 11)
    key_off, key_extra, key_block = jax.random.split(key, 3)
    offset = jax.random.randint(key_off, (), 1, PAGE)
    places = jnp.arange(TOKENS, dtype=jnp.int32)
    forced = (places % PAGE == offset) | (places == 0)
    extra = jax.random.randint(key_extra, (TOKENS,), 0, max(2, PAGE // 4)) == 0
    extra = extra & (places % TOK_DEV != 0)
    chosen = jax.random.randint(key_block, (), 0, TOKENS // PAGE - 1)
    lower = chosen * PAGE + offset
    inside = (places > lower) & (places < lower + PAGE)
    bound = forced | extra & jnp.logical_not(inside)
    return lax.cummax(jnp.where(bound, places, 0), axis=0).astype(jnp.int32)


def steps_of(stream_key, shape, pieces, low, top_value):
    def one(position, shards_of):
        steps = jax.random.uniform(jax.random.fold_in(jax.random.fold_in(stream_key, 6), position), (shards_of,), jnp.float32, low / len(pieces), top_value / len(pieces))
        return jnp.repeat(jnp.exp(steps), shape[position] // shards_of).reshape((-1,) + (1,) * (len(shape) - position - 1))

    loudness = one(*pieces[0])
    for cut in pieces[1:]:
        loudness = loudness * one(*cut)
    return loudness


def bell_draw(own_key, dims, scale, limit, shards=(), kind=jnp.bfloat16):
    entries = scale * jax.random.normal(own_key, dims, jnp.float32)
    if shards:
        entries = entries * steps_of(own_key, dims, shards, -0.22, 0.18)
    return jnp.clip(entries, -limit, limit).astype(kind)


def setup_inputs(seed: int = 0, part: int = 0) -> dict:
    arg_keys = jax.random.split(jax.random.key(seed), 5)
    part_splits = jax.random.split(jax.random.fold_in(arg_keys[4], part), 5)
    queries = draw_queries(jax.random.fold_in(jax.random.fold_in(arg_keys[4], part), 71), part)
    keys = draw_keys(jax.random.fold_in(jax.random.fold_in(arg_keys[4], part), 71), part)
    values = bell_draw(part_splits[2], (TOKENS, KV_HEADS * HD), 1.0, 6.0, ((0, 4),))
    page_start = draw_page_start(jax.random.fold_in(jax.random.fold_in(arg_keys[4], part), 71), part)
    return {"queries": queries, "keys": keys, "values": values, "page_start": page_start}


def reference(queries, keys, values, page_start):
    tokens = queries.shape[0]
    group = HEADS // KV_HEADS
    scale = 1.0 / (HD ** 0.5)
    zeros = jnp.zeros((PAGE, KV_HEADS * HD), jnp.bfloat16)
    key_pad = jnp.concatenate([zeros, keys], 0)
    value_pad = jnp.concatenate([zeros, values], 0)

    def attend(block):
        first = (block * PAGE).astype(jnp.int32)
        query_rows = lax.dynamic_slice_in_dim(queries, first, PAGE, 0)
        query_rows = query_rows.astype(jnp.float32).reshape(PAGE, KV_HEADS, group, HD)
        key_rows = lax.dynamic_slice_in_dim(key_pad, first, 2 * PAGE, 0).astype(jnp.float32).reshape(2 * PAGE, KV_HEADS, HD)
        value_rows = lax.dynamic_slice_in_dim(value_pad, first, 2 * PAGE, 0).astype(jnp.float32).reshape(2 * PAGE, KV_HEADS, HD)
        scores = jnp.einsum("qkgd,skd->kgqs", query_rows, key_rows) * scale
        query_pos = first + jnp.arange(PAGE, dtype=jnp.int32)
        key_pos = first - PAGE + jnp.arange(2 * PAGE, dtype=jnp.int32)
        starts = lax.dynamic_slice_in_dim(page_start, first, PAGE, 0)
        visible = (key_pos[None, :] >= starts[:, None]) & (key_pos[None, :] <= query_pos[:, None])
        scores = jnp.where(visible[None, None], scores, -1e30)
        top = jnp.max(scores, axis=-1, keepdims=True)
        expo = jnp.exp(scores - top)
        probs = (expo / jnp.sum(expo, axis=-1, keepdims=True)).astype(jnp.bfloat16)
        mixed = jnp.einsum("kgqs,skd->qkgd", probs.astype(jnp.float32), value_rows)
        return mixed.reshape(PAGE, HEADS * HD).astype(jnp.bfloat16)

    attn = lax.map(attend, jnp.arange(tokens // PAGE, dtype=jnp.int32)).reshape(tokens, HEADS * HD)
    width = HEADS * HD // N_TENSOR
    steps = N_TENSOR // 2 + 1
    doubled = jnp.concatenate([attn, attn], 1)
    runs = tokens // N_DP

    def band_rows(index):
        first = (index * width).astype(jnp.int32)
        rows = lax.dynamic_slice_in_dim(attn, first, width, 1).reshape(N_DP, runs, width)
        cols = lax.dynamic_slice_in_dim(doubled, first, steps * width, 1).reshape(N_DP, runs, steps * width)
        partial_value = jnp.einsum("ntr,ntc->nrc", rows.astype(jnp.float32), cols.astype(jnp.float32))
        rounded = lax.optimization_barrier(partial_value.astype(jnp.bfloat16))
        return jnp.sum(rounded.astype(jnp.float32), axis=0) * (2.0 / tokens)

    band = lax.map(band_rows, jnp.arange(N_TENSOR, dtype=jnp.int32))
    return band.reshape(HEADS * HD, steps * width)
```

```python
import functools

import jax
import jax.numpy as jnp
from jax import lax
from jax.experimental import pallas as pl
from jax.experimental.pallas import tpu as pltpu
from jax.sharding import PartitionSpec as P

HEADS = 96
HD = 128
KV_HEADS = 8
PAGE = 512
TILE = 256
LOG2E = 1.4426950408889634
VMEM_LIMIT = 56 * 1024 * 1024


def shifted(x, axis, by):
    devices = lax.axis_size(axis)
    pairs = [(i, i + by) for i in range(devices) if 0 <= i + by < devices]
    return lax.ppermute(x, axis, pairs)


def from_behind(value, axis, steps):
    count = lax.axis_size(axis)
    pairs = [(source, (source + steps) % count) for source in range(count)]
    return lax.ppermute(value, axis, pairs)


def attend_kernel(start_ref, q_ref, kp_ref, ko_ref, vp_ref, vo_ref, out_ref, bias_ref):
    rows = q_ref.shape[0]
    tiles = rows // TILE
    keys_seen = PAGE + TILE

    @pl.when(pl.program_id(0) == 0)
    def _():
        for tile in range(tiles):
            shape = (TILE, keys_seen)
            query = lax.broadcasted_iota(jnp.int32, shape, 0) + tile * TILE
            key = lax.broadcasted_iota(jnp.int32, shape, 1) + (tile * TILE - PAGE)
            first = start_ref[tile * TILE : (tile + 1) * TILE, :]
            visible = (key >= first) & (key <= query)
            bias_ref[tile] = jnp.where(visible, 0.0, -1e30)

    for tile in range(tiles):
        lo = tile * TILE
        query = q_ref[lo : lo + TILE, :]
        parts_k = [kp_ref[lo:, :], ko_ref[: lo + TILE, :]]
        parts_v = [vp_ref[lo:, :], vo_ref[: lo + TILE, :]]
        key = jnp.concatenate(parts_k, 0)
        value = jnp.concatenate(parts_v, 0)
        scores = lax.dot_general(
            query, key, (((1,), (1,)), ((), ())), preferred_element_type=jnp.float32
        )
        scores = scores + bias_ref[tile]
        top = jnp.max(scores, axis=-1, keepdims=True)
        expo = jnp.exp2((scores - top) * (LOG2E / HD**0.5))
        total = jnp.sum(expo, axis=-1, keepdims=True)
        mixed = jnp.dot(expo.astype(jnp.bfloat16), value, preferred_element_type=jnp.float32)
        out_ref[lo : lo + TILE, :] = (mixed / total).astype(jnp.bfloat16)


def attend(queries, prev_kv, own_kv, start, first_head, heads, per_kv):
    rows = queries.shape[0]
    kv_spec = pl.BlockSpec((PAGE, HD), lambda h: (0, (first_head + h) // per_kv))
    return pl.pallas_call(
        attend_kernel,
        grid=(heads,),
        out_shape=jax.ShapeDtypeStruct((rows, heads * HD), jnp.bfloat16),
        in_specs=[
            pl.BlockSpec((rows, 1), lambda h: (0, 0)),
            pl.BlockSpec((rows, HD), lambda h: (0, first_head + h)),
            kv_spec,
            kv_spec,
            kv_spec,
            kv_spec,
        ],
        out_specs=pl.BlockSpec((rows, HD), lambda h: (0, h)),
        scratch_shapes=[pltpu.VMEM((rows // TILE, TILE, PAGE + TILE), jnp.float32)],
        compiler_params=pltpu.CompilerParams(vmem_limit_bytes=VMEM_LIMIT),
        cost_estimate=pl.CostEstimate(
            flops=heads * rows * (PAGE + TILE) * HD * 8,
            bytes_accessed=heads * rows * HD * 4,
            transcendentals=heads * rows * (PAGE + TILE),
        ),
    )(start, queries, prev_kv[0], own_kv[0], prev_kv[1], own_kv[1])


def gram_kernel(runs, widths, kinds, depth, rows, scale, has_acc, *refs):
    chunks = len(widths)
    offsets = [sum(widths[:c]) for c in range(chunks)]
    block = sum(widths)
    place_ref = refs[0]
    data = refs[1 : 1 + runs * kinds * chunks]
    rest = list(refs[1 + runs * kinds * chunks :])
    acc_ref = rest.pop(0) if has_acc else None
    out_ref = rest.pop(0)
    a_raw, a_t, b_buf, o_buf, a_sem, b_sem, o_sem = rest[:7]
    c_buf, c_sem = rest[7:] if has_acc else (None, None)

    def source(run, kind, chunk):
        return data[(run * kinds + kind) * chunks + chunk]

    tiles = [(k, c) for k in range(kinds) for c in range(chunks)]

    def b_copies(i):
        kind, chunk = tiles[i]
        slot = i % 2
        return [
            pltpu.make_async_copy(
                source(run, kind, chunk),
                b_buf.at[slot, pl.ds(run * depth, depth), pl.ds(0, widths[chunk])],
                b_sem.at[slot, run],
            )
            for run in range(runs)
        ]

    def columns(i):
        kind, chunk = tiles[i]
        return pl.ds(kind * block + offsets[chunk], widths[chunk])

    def c_copy(i):
        slot = i % 2
        return pltpu.make_async_copy(
            acc_ref.at[:, columns(i)],
            c_buf.at[slot, :, pl.ds(0, widths[tiles[i][1]])],
            c_sem.at[slot],
        )

    def o_copy(i):
        slot = i % 2
        return pltpu.make_async_copy(
            o_buf.at[slot, :, pl.ds(0, widths[tiles[i][1]])],
            out_ref.at[:, columns(i)],
            o_sem.at[slot],
        )

    def start(i):
        for copy in b_copies(i):
            copy.start()
        if has_acc:
            c_copy(i).start()

    place = place_ref[0]
    for where in range(block // rows):

        @pl.when(place == where)
        def _():
            lo, hi = where * rows, (where + 1) * rows
            copies = []
            for run in range(runs):
                piece = 0
                for chunk in range(chunks):
                    first = max(lo, offsets[chunk])
                    last = min(hi, offsets[chunk] + widths[chunk])
                    if first >= last:
                        continue
                    copies.append(
                        pltpu.make_async_copy(
                            source(run, 0, chunk).at[:, pl.ds(first - offsets[chunk], last - first)],
                            a_raw.at[pl.ds(run * depth, depth), pl.ds(first - lo, last - first)],
                            a_sem.at[run, piece],
                        )
                    )
                    piece += 1
            for copy in copies:
                copy.start()
            for copy in copies:
                copy.wait()

    start(0)
    a_t[...] = a_raw[...].T
    for i, (kind, chunk) in enumerate(tiles):
        slot = i % 2
        width = widths[chunk]
        if i + 1 < len(tiles):
            start(i + 1)
        for copy in b_copies(i):
            copy.wait()
        if i >= 2:
            o_copy(i - 2).wait()
        result = scale * jnp.dot(
            a_t[...], b_buf[slot, :, :width], preferred_element_type=jnp.float32
        )
        if has_acc:
            c_copy(i).wait()
            result = result + c_buf[slot, :, :width]
        o_buf[slot, :, :width] = result
        o_copy(i).start()
    for i in range(max(0, len(tiles) - 2), len(tiles)):
        o_copy(i).wait()


def gram(place, sources, rows, scale, acc=None):
    runs, kinds, chunks = len(sources), len(sources[0]), len(sources[0][0])
    widths = tuple(x.shape[1] for x in sources[0][0])
    depth = sources[0][0][0].shape[0]
    block = sum(widths)
    wide = max(widths)
    data = [x for run in sources for kind in run for x in kind]
    has_acc = acc is not None
    any_spec = pl.BlockSpec(memory_space=pl.ANY)
    operands = [place, *data] + ([acc] if has_acc else [])
    scratch = [
        pltpu.VMEM((runs * depth, rows), jnp.bfloat16),
        pltpu.VMEM((rows, runs * depth), jnp.bfloat16),
        pltpu.VMEM((2, runs * depth, wide), jnp.bfloat16),
        pltpu.VMEM((2, rows, wide), jnp.float32),
        pltpu.SemaphoreType.DMA((runs, chunks)),
        pltpu.SemaphoreType.DMA((2, runs)),
        pltpu.SemaphoreType.DMA((2,)),
    ]
    if has_acc:
        scratch += [pltpu.VMEM((2, rows, wide), jnp.float32), pltpu.SemaphoreType.DMA((2,))]
    return pl.pallas_call(
        functools.partial(gram_kernel, runs, widths, kinds, depth, rows, scale, has_acc),
        out_shape=jax.ShapeDtypeStruct((rows, kinds * block), jnp.float32),
        in_specs=[pl.BlockSpec(memory_space=pltpu.SMEM)] + [any_spec] * (len(operands) - 1),
        out_specs=any_spec,
        scratch_shapes=scratch,
        input_output_aliases={len(operands) - 1: 0} if has_acc else {},
        compiler_params=pltpu.CompilerParams(vmem_limit_bytes=VMEM_LIMIT),
        cost_estimate=pl.CostEstimate(
            flops=2 * runs * depth * rows * kinds * block,
            bytes_accessed=runs * depth * kinds * block * 2 + rows * kinds * block * (8 if has_acc else 4),
            transcendentals=0,
        ),
    )(*operands)


def own_kv_of(keys, values, local_heads):
    group = HEADS // KV_HEADS
    kv_count = max(1, local_heads // group)
    kv_first = lax.axis_index("tensor") * local_heads // group
    own_keys = lax.dynamic_slice_in_dim(keys, kv_first * HD, kv_count * HD, 1)
    own_values = lax.dynamic_slice_in_dim(values, kv_first * HD, kv_count * HD, 1)
    return (own_keys, own_values), kv_count


def per_device(queries, keys, values, page_start):
    tok_rows, slab_width = queries.shape
    local_heads = slab_width // HD
    runs = lax.axis_size("dp")
    own_kv, kv_count = own_kv_of(keys, values, local_heads)
    prev_kv = shifted(own_kv, "dp", 1)
    run_index = lax.axis_index("dp")
    start = (page_start - run_index * tok_rows).reshape(tok_rows, 1)
    per_kv = local_heads // kv_count

    size = local_heads // 6
    chunks = [(c * size, size) for c in range(6)]
    mirror_first = 1
    own = [[attend(queries, prev_kv, own_kv, start, h, n, per_kv)] for h, n in chunks]
    mirror = [[lax.ppermute(x[0], "tensor", [(t, t ^ 2) for t in range(4)])] for x in own]
    order = list(range(mirror_first, len(chunks))) + list(range(mirror_first))
    for _ in range(1, runs):
        for c in order:
            own[c].append(from_behind(own[c][-1], "dp", 1))
            if c < mirror_first:
                mirror[c].append(from_behind(mirror[c][-1], "dp", 1))
            else:
                mirror[c].append(lax.ppermute(own[c][-1], "tensor", [(t, t ^ 2) for t in range(4)]))
    even = lax.axis_index("tensor") % 2 == 0
    sibling = [
        [
            lax.ppermute(
                jnp.where(even, mirror[c][r], own[c][r]), "tensor", [(t, t ^ 1) for t in range(4)]
            )
            for r in range(runs)
        ]
        for c in range(len(chunks))
    ]

    def run_of(r):
        return [[x[r] for x in own], [x[r] for x in sibling], [x[r] for x in mirror]]

    rows = slab_width // runs
    scale = 2.0 / (tok_rows * runs)
    place = run_index.reshape(1)
    acc = gram(place, [run_of(r) for r in range(runs - 1)], rows, scale)
    return gram(place, [run_of(runs - 1)], rows, scale, acc)


def per_device_general(queries, keys, values, page_start):
    tok_rows, slab_width = queries.shape
    local_heads = slab_width // HD
    runs = lax.axis_size("dp")
    own_kv, kv_count = own_kv_of(keys, values, local_heads)
    prev_kv = shifted(own_kv, "dp", 1)
    run_index = lax.axis_index("dp")
    start = (page_start - run_index * tok_rows).reshape(tok_rows, 1)
    outputs = attend(queries, prev_kv, own_kv, start, 0, local_heads, local_heads // kv_count)
    steps = lax.axis_size("tensor") // 2 + 1
    rows = slab_width // runs
    moving = lax.all_gather(outputs, "dp", axis=0, tiled=True)
    left = lax.dynamic_slice_in_dim(moving, run_index * rows, rows, 1)
    tiles = []
    for offset in range(steps):
        if offset:
            moving = from_behind(moving, "tensor", -1)
        tiles.append(
            lax.dot_general(
                left, moving, (((0,), (0,)), ((), ())), preferred_element_type=jnp.float32
            )
        )
    return jnp.concatenate(tiles, 1) * (2.0 / (tok_rows * runs))


def solution(mesh):
    cores = mesh.shape["tensor"]
    rows = HEADS * HD // cores // mesh.shape["dp"]
    tuned = cores == 4 and rows % HD == 0
    return jax.shard_map(
        per_device if tuned else per_device_general,
        mesh=mesh,
        in_specs=(
            P(("groups", "dp"), "tensor"),
            P(("groups", "dp"), None),
            P(("groups", "dp"), None),
            P(("groups", "dp")),
        ),
        out_specs=P(("groups", "tensor", "dp"), None),
        check_vma=False,
    )
```

```python
import functools

import jax
import jax.numpy as jnp
from jax import lax
from jax.experimental import pallas as pl
from jax.experimental.pallas import tpu as pltpu
from jax.sharding import PartitionSpec as P

HEADS = 96
HD = 128
KV_HEADS = 8
PAGE = 512
TILE = 256
LOG2E = 1.4426950408889634
VMEM_LIMIT = 56 * 1024 * 1024


def shifted(x, axis, by):
    devices = lax.axis_size(axis)
    pairs = [(i, i + by) for i in range(devices) if 0 <= i + by < devices]
    return lax.ppermute(x, axis, pairs)


def from_behind(value, axis, steps):
    count = lax.axis_size(axis)
    pairs = [(source, (source + steps) % count) for source in range(count)]
    return lax.ppermute(value, axis, pairs)


def over_tensor(value, bit):
    count = lax.axis_size("tensor")
    return lax.ppermute(value, "tensor", [(t, t ^ bit) for t in range(count)])


def tie(value, *after):
    return lax.optimization_barrier((value, *after))[0] if after else value


def held(value, out, *after):
    if out is None:
        return tie(value, *after), None
    return lax.optimization_barrier((value, out, *after))[:2]


def attend_kernel(start_ref, q_ref, kp_ref, ko_ref, vp_ref, vo_ref, out_ref, bias_ref):
    rows = q_ref.shape[0]
    tiles = rows // TILE
    keys_seen = PAGE + TILE

    @pl.when(pl.program_id(0) == 0)
    def _():
        for tile in range(tiles):
            shape = (TILE, keys_seen)
            query = lax.broadcasted_iota(jnp.int32, shape, 0) + tile * TILE
            key = lax.broadcasted_iota(jnp.int32, shape, 1) + (tile * TILE - PAGE)
            first = start_ref[tile * TILE : (tile + 1) * TILE, :]
            visible = (key >= first) & (key <= query)
            bias_ref[tile] = jnp.where(visible, 0.0, -1e30)

    for tile in range(tiles):
        lo = tile * TILE
        query = q_ref[lo : lo + TILE, :]
        parts_k = [kp_ref[lo:, :], ko_ref[: lo + TILE, :]]
        parts_v = [vp_ref[lo:, :], vo_ref[: lo + TILE, :]]
        key = jnp.concatenate(parts_k, 0)
        value = jnp.concatenate(parts_v, 0)
        scores = lax.dot_general(
            query, key, (((1,), (1,)), ((), ())), preferred_element_type=jnp.float32
        )
        scores = scores + bias_ref[tile]
        top = jnp.max(scores, axis=-1, keepdims=True)
        expo = jnp.exp2((scores - top) * (LOG2E / HD**0.5))
        total = jnp.sum(expo, axis=-1, keepdims=True)
        mixed = jnp.dot(expo.astype(jnp.bfloat16), value, preferred_element_type=jnp.float32)
        out_ref[lo : lo + TILE, :] = (mixed / total).astype(jnp.bfloat16)


def attend(queries, own_kv, prev_kv, start, first_head, heads):
    rows = queries.shape[0]
    key_spec = pl.BlockSpec((PAGE, HD), lambda h: (0, 0))
    value_spec = pl.BlockSpec((PAGE, HD), lambda h: (0, 1))
    return pl.pallas_call(
        attend_kernel,
        grid=(heads,),
        out_shape=jax.ShapeDtypeStruct((rows, heads * HD), jnp.bfloat16),
        in_specs=[
            pl.BlockSpec((rows, 1), lambda h: (0, 0)),
            pl.BlockSpec((rows, HD), lambda h: (0, first_head + h)),
            key_spec,
            key_spec,
            value_spec,
            value_spec,
        ],
        out_specs=pl.BlockSpec((rows, HD), lambda h: (0, h)),
        scratch_shapes=[pltpu.VMEM((rows // TILE, TILE, PAGE + TILE), jnp.float32)],
        compiler_params=pltpu.CompilerParams(vmem_limit_bytes=VMEM_LIMIT),
        cost_estimate=pl.CostEstimate(flops=10**15, bytes_accessed=1, transcendentals=0),
    )(start, queries, prev_kv, own_kv, prev_kv, own_kv)


def rows_kernel(widths, rows, place_ref, *refs):
    chunks = len(widths)
    sources, (out_ref, raw, sem) = refs[:chunks], refs[chunks:]
    offsets = [sum(widths[:c]) for c in range(chunks)]
    for where in range(sum(widths) // rows):

        @pl.when(place_ref[0] == where)
        def _():
            lo, hi = where * rows, (where + 1) * rows
            copies = []
            for c in range(chunks):
                first, last = max(lo, offsets[c]), min(hi, offsets[c] + widths[c])
                if first < last:
                    copies.append(
                        pltpu.make_async_copy(
                            sources[c].at[:, pl.ds(first - offsets[c], last - first)],
                            raw.at[:, pl.ds(first - lo, last - first)],
                            sem.at[len(copies)],
                        )
                    )
            for copy in copies:
                copy.start()
            for copy in copies:
                copy.wait()

    out_ref[...] = raw[...].T


def rows_of(place, pieces, rows):
    depth = pieces[0].shape[0]
    widths = tuple(x.shape[1] for x in pieces)
    return pl.pallas_call(
        functools.partial(rows_kernel, widths, rows),
        out_shape=jax.ShapeDtypeStruct((rows, depth), jnp.bfloat16),
        in_specs=[pl.BlockSpec(memory_space=pltpu.SMEM)]
        + [pl.BlockSpec(memory_space=pltpu.HBM)] * len(pieces),
        scratch_shapes=[
            pltpu.VMEM((depth, rows), jnp.bfloat16),
            pltpu.SemaphoreType.DMA((len(pieces),)),
        ],
        compiler_params=pltpu.CompilerParams(vmem_limit_bytes=VMEM_LIMIT),
        cost_estimate=pl.CostEstimate(flops=10**15, bytes_accessed=1, transcendentals=0),
    )(place, *pieces)


def gram_kernel(runs, tiles, starts, depth, scale, kept, added, *refs):
    lefts, refs = refs[:runs], refs[runs:]
    data, refs = refs[: runs * len(tiles)], list(refs[runs * len(tiles) :])
    old_ref = refs.pop(0) if kept else None
    out_ref, left, b_buf, o_buf, left_sem, b_sem, o_sem = refs[:7]
    c_buf, c_sem = refs[7:] if added else (None, None)
    slots = b_buf.shape[0]

    def in_copies(i):
        slot = i % slots
        width = tiles[i][1]
        copies = [
            pltpu.make_async_copy(
                data[i * runs + run].at[:, pl.ds(starts[i * runs + run], width)],
                b_buf.at[slot, pl.ds(run * depth, depth), pl.ds(0, width)],
                b_sem.at[slot, run],
            )
            for run in range(runs)
        ]
        if added:
            copies.append(
                pltpu.make_async_copy(
                    old_ref.at[:, pl.ds(*tiles[i])],
                    c_buf.at[slot, :, pl.ds(0, width)],
                    c_sem.at[slot],
                )
            )
        return copies

    def out_copy(i):
        slot = i % slots
        return pltpu.make_async_copy(
            o_buf.at[slot, :, pl.ds(0, tiles[i][1])],
            out_ref.at[:, pl.ds(*tiles[i])],
            o_sem.at[slot],
        )

    left_copies = [
        pltpu.make_async_copy(
            lefts[run], left.at[:, pl.ds(run * depth, depth)], left_sem.at[run]
        )
        for run in range(runs)
    ]
    for copy in left_copies + in_copies(0):
        copy.start()
    for copy in left_copies:
        copy.wait()
    for i in range(1, min(slots - 1, len(tiles))):
        for copy in in_copies(i):
            copy.start()
    for i, (_, width) in enumerate(tiles):
        slot = i % slots
        if i + slots - 1 < len(tiles):
            for copy in in_copies(i + slots - 1):
                copy.start()
        for copy in in_copies(i):
            copy.wait()
        if i >= slots:
            out_copy(i - slots).wait()
        result = scale * jnp.dot(
            left[...], b_buf[slot, :, :width], preferred_element_type=jnp.float32
        )
        if added:
            result = result + c_buf[slot, :, :width]
        o_buf[slot, :, :width] = result
        out_copy(i).start()
    for i in range(max(0, len(tiles) - slots), len(tiles)):
        out_copy(i).wait()


def gram(out, lefts, tiles, width, columns, scale, added=False):
    runs = len(lefts)
    rows, depth = lefts[0].shape
    places = [(first, width) for first, _ in tiles]
    data = [x for _, arrays in tiles for x, _ in arrays]
    starts = [x for _, arrays in tiles for _, x in arrays]
    kept = out is not None
    any_spec = pl.BlockSpec(memory_space=pltpu.HBM)
    operands = [*lefts, *data] + ([out] if kept else [])
    slots = min(4, len(tiles))
    scratch = [
        pltpu.VMEM((rows, runs * depth), jnp.bfloat16),
        pltpu.VMEM((slots, runs * depth, width), jnp.bfloat16),
        pltpu.VMEM((slots, rows, width), jnp.float32),
        pltpu.SemaphoreType.DMA((runs,)),
        pltpu.SemaphoreType.DMA((slots, runs)),
        pltpu.SemaphoreType.DMA((slots,)),
    ]
    if added:
        scratch += [pltpu.VMEM((slots, rows, width), jnp.float32), pltpu.SemaphoreType.DMA((slots,))]
    total = sum(width for _, width in places)
    return pl.pallas_call(
        functools.partial(gram_kernel, runs, places, starts, depth, scale, kept, added),
        out_shape=jax.ShapeDtypeStruct((rows, columns), jnp.float32),
        in_specs=[any_spec] * len(operands),
        out_specs=any_spec,
        scratch_shapes=scratch,
        input_output_aliases={len(operands) - 1: 0} if kept else {},
        compiler_params=pltpu.CompilerParams(vmem_limit_bytes=VMEM_LIMIT),
        cost_estimate=pl.CostEstimate(flops=10**15, bytes_accessed=1, transcendentals=0),
    )(*operands)


def kv_of(keys, values, local_heads):
    group = HEADS // KV_HEADS
    kv_count = max(1, local_heads // group)
    kv_first = lax.axis_index("tensor") * local_heads // group
    own, prev = [], []
    for k in range(kv_count):
        parts = [lax.dynamic_slice_in_dim(x, (kv_first + k) * HD, HD, 1) for x in (keys, values)]
        own.append(jnp.concatenate(parts, 1))
        prev.append(shifted(own[k], "dp", 1))
    return list(zip(own, prev)), local_heads // kv_count


CHUNKS = 6


def per_device(queries, keys, values, page_start):
    tok_rows, slab = queries.shape
    local_heads = slab // HD
    runs = lax.axis_size("dp")
    kv, per_kv = kv_of(keys, values, local_heads)
    run_index = lax.axis_index("dp")
    start = (page_start - run_index * tok_rows).reshape(tok_rows, 1)
    place = run_index.reshape(1)
    rows = slab // runs
    scale = 2.0 / (tok_rows * runs)
    even = lax.axis_index("tensor") % 2 == 0

    size = local_heads // CHUNKS
    width = size * HD
    own, mirror, sibling = {}, {}, {}
    within = {}
    half = CHUNKS // 2
    last = runs - 1
    over_z = [("own", c, r) for r in range(1, runs) for c in range(CHUNKS)]
    over_z += [("mirror", c, last) for c in range(half, CHUNKS)]
    over_y = [(c, r) for r in range(last) for c in range(CHUNKS)]
    over_y += [(c, last) for c in range(half)]

    left = {}
    out = None
    steps = max(len(over_z), len(over_y))
    ended = {}
    swapped = []
    def tiles(kinds, chosen, some_runs):
        tables = (own, sibling, mirror)
        return [
            (
                k * slab + c * width,
                [(tables[k][c, r], within[c, r] if k == 1 else 0) for r in some_runs],
            )
            for c in chosen
            for k in kinds
        ]

    def rows_for(some_runs):
        for r in some_runs:
            if r not in left:
                left[r] = rows_of(place, [own[c, r] for c in range(CHUNKS)], rows)
        return [left[r] for r in some_runs]

    every = list(range(runs))
    everything = list(range(CHUNKS))
    first_runs, last_runs = every[: runs // 2], every[runs // 2 :]
    moved = (2, 1)
    done = last * CHUNKS
    work = {
        done - 12: [("rows", 0)],
        done - 11: [("rows", 1)],
        done - 10: [((0,), everything, first_runs, False)],
        done - 8: [(moved, [0, 1], first_runs, False)],
        done - 6: [(moved, [2, 3], first_runs, False)],
        done - 4: [(moved, [4, 5], first_runs, False)],
        done - 2: [("rows", 2)],
        done + 1: [("rows", 3)],
        done + 2: [((0,), everything, last_runs, True)],
        done + 3: [(moved, [0, half], last_runs, True)],
        done + 4: [(moved, [1, half + 1], last_runs, True)],
        done + 5: [(moved, [half - 1, CHUNKS - 1], last_runs, True)],
    }

    for step in range(steps + 3):
        before = ended.get(step - 2, [])
        if step < CHUNKS:
            first = step * size
            some = tie(start, *[prev for _, prev in kv]) if step == 1 else start
            own[step, 0] = attend(queries, *kv[first // per_kv], some, first, size)
        arrived = []
        if step < len(over_z):
            kind, c, r = over_z[step]
            table = own if kind == "own" else mirror
            value, out = held(table[c, r - 1], out, *before)
            table[c, r] = from_behind(value, "dp", 1)
            arrived.append(table[c, r])
        if step < len(over_y):
            c, r = over_y[step]
            value, out = held(own[c, r], out, *before)
            mirror[c, r] = over_tensor(value, 2)
            arrived.append(mirror[c, r])
        ended[step] = arrived
        past = step - 2
        swaps = over_y[past : past + 1] if past >= 0 else []
        swaps = swaps + [x[1:] for x in over_z[max(past, 0) : max(past + 1, 0)] if x[0] == "mirror"]
        if swaps:
            pair = ([mirror[x] for x in swaps], [own[x] for x in swaps])
            pair, out = held(pair, out, *before, *swapped)
            sent = jnp.where(even, *[jnp.concatenate(x, 1) for x in pair])
            sent = over_tensor(sent, 1)
            swapped = [sent]
            sibling.update({x: sent for x in swaps})
            within.update({x: i * width for i, x in enumerate(swaps)})
        for job in work.pop(step, ()):
            if job[0] == "rows":
                ended[step] += rows_for([job[1]])
            else:
                kinds, chosen, some_runs, added = job
                lefts, pieces = rows_for(some_runs), tiles(kinds, chosen, some_runs)
                out = gram(out, lefts, pieces, width, 3 * slab, scale, added)
    assert not work
    return out


def per_device_general(queries, keys, values, page_start):
    tok_rows, slab_width = queries.shape
    local_heads = slab_width // HD
    runs = lax.axis_size("dp")
    kv, per_kv = kv_of(keys, values, local_heads)
    run_index = lax.axis_index("dp")
    start = (page_start - run_index * tok_rows).reshape(tok_rows, 1)
    outputs = jnp.concatenate(
        [attend(queries, *kv[h // per_kv], start, h, per_kv) for h in range(0, local_heads, per_kv)], 1
    )
    steps = lax.axis_size("tensor") // 2 + 1
    rows = slab_width // runs
    moving = lax.all_gather(outputs, "dp", axis=0, tiled=True)
    left = lax.dynamic_slice_in_dim(moving, run_index * rows, rows, 1)
    tiles = []
    for offset in range(steps):
        if offset:
            moving = from_behind(moving, "tensor", -1)
        tiles.append(
            lax.dot_general(
                left, moving, (((0,), (0,)), ((), ())), preferred_element_type=jnp.float32
            )
        )
    return jnp.concatenate(tiles, 1) * (2.0 / (tok_rows * runs))


def solution(mesh):
    cores = mesh.shape["tensor"]
    rows = HEADS * HD // cores // mesh.shape["dp"]
    tuned = cores == 4 and rows % HD == 0
    return jax.shard_map(
        per_device if tuned else per_device_general,
        mesh=mesh,
        in_specs=(
            P(("groups", "dp"), "tensor"),
            P(("groups", "dp"), None),
            P(("groups", "dp"), None),
            P(("groups", "dp")),
        ),
        out_specs=P(("groups", "tensor", "dp"), None),
        check_vma=False,
    )
```

```python
import functools

import jax
import jax.numpy as jnp
from jax import lax
from jax.experimental import pallas as pl
from jax.experimental.pallas import tpu as pltpu
from jax.sharding import PartitionSpec as P

HEADS = 96
HD = 128
KV_HEADS = 8
PAGE = 512
TILE = 256
STEP = 4
LOG2E = 1.4426950408889634
VMEM_LIMIT = 56 * 1024 * 1024


def shifted(x, axis, by):
    devices = lax.axis_size(axis)
    pairs = [(i, i + by) for i in range(devices) if 0 <= i + by < devices]
    return lax.ppermute(x, axis, pairs)


def from_behind(value, axis, steps):
    count = lax.axis_size(axis)
    pairs = [(source, (source + steps) % count) for source in range(count)]
    return lax.ppermute(value, axis, pairs)


def over_tensor(value, bit):
    count = lax.axis_size("tensor")
    return lax.ppermute(value, "tensor", [(t, t ^ bit) for t in range(count)])


def tie(value, *after):
    return lax.optimization_barrier((value, *after))[0] if after else value


def held(value, sums, *after):
    return lax.optimization_barrier((value, sums, *after))[:2]


def attend_kernel(start_ref, q_ref, kp_ref, ko_ref, vp_ref, vo_ref, out_ref, bias_ref):
    rows = q_ref.shape[0]
    tiles = rows // TILE
    keys_seen = PAGE + TILE

    @pl.when(pl.program_id(0) == 0)
    def _():
        for tile in range(tiles):
            shape = (TILE, keys_seen)
            query = lax.broadcasted_iota(jnp.int32, shape, 0) + tile * TILE
            key = lax.broadcasted_iota(jnp.int32, shape, 1) + (tile * TILE - PAGE)
            first = start_ref[tile * TILE : (tile + 1) * TILE, :]
            visible = (key >= first) & (key <= query)
            bias_ref[tile] = jnp.where(visible, 0.0, -1e30)

    for tile in range(tiles):
        lo = tile * TILE
        key = jnp.concatenate([kp_ref[lo:, :], ko_ref[: lo + TILE, :]], 0)
        value = jnp.concatenate([vp_ref[lo:, :], vo_ref[: lo + TILE, :]], 0)
        value = jnp.concatenate([value, jnp.ones_like(value)], 1)
        for head in range(q_ref.shape[1] // HD):
            columns = slice(head * HD, (head + 1) * HD)
            scores = lax.dot_general(
                q_ref[lo : lo + TILE, columns],
                key,
                (((1,), (1,)), ((), ())),
                preferred_element_type=jnp.float32,
            )
            scores = scores + bias_ref[tile]
            top = jnp.max(scores, axis=-1, keepdims=True)
            expo = jnp.exp2((scores - top) * (LOG2E / HD**0.5)).astype(jnp.bfloat16)
            mixed = jnp.dot(expo, value, preferred_element_type=jnp.float32)
            out_ref[lo : lo + TILE, columns] = (mixed[:, :HD] / mixed[:, HD:]).astype(jnp.bfloat16)


def attend(queries, own_kv, prev_kv, start, first_head, heads):
    rows = queries.shape[0]
    step = STEP if heads % STEP == 0 and first_head % STEP == 0 else 1
    key_spec = pl.BlockSpec((PAGE, HD), lambda h: (0, 0))
    value_spec = pl.BlockSpec((PAGE, HD), lambda h: (0, 1))
    return pl.pallas_call(
        attend_kernel,
        grid=(heads // step,),
        out_shape=jax.ShapeDtypeStruct((rows, heads * HD), jnp.bfloat16),
        in_specs=[
            pl.BlockSpec((rows, 1), lambda h: (0, 0)),
            pl.BlockSpec((rows, step * HD), lambda h: (0, first_head // step + h)),
            key_spec,
            key_spec,
            value_spec,
            value_spec,
        ],
        out_specs=pl.BlockSpec((rows, step * HD), lambda h: (0, h)),
        scratch_shapes=[pltpu.VMEM((rows // TILE, TILE, PAGE + TILE), jnp.float32)],
        compiler_params=pltpu.CompilerParams(vmem_limit_bytes=VMEM_LIMIT),
        cost_estimate=pl.CostEstimate(flops=10**15, bytes_accessed=1, transcendentals=0),
    )(start, queries, prev_kv, own_kv, prev_kv, own_kv)


def rows_kernel(widths, rows, place_ref, *refs):
    chunks = len(widths)
    sources, (out_ref, raw, sem) = refs[:chunks], refs[chunks:]
    offsets = [sum(widths[:c]) for c in range(chunks)]
    for where in range(sum(widths) // rows):

        @pl.when(place_ref[0] == where)
        def _():
            lo, hi = where * rows, (where + 1) * rows
            copies = []
            for c in range(chunks):
                first, last = max(lo, offsets[c]), min(hi, offsets[c] + widths[c])
                if first < last:
                    copies.append(
                        pltpu.make_async_copy(
                            sources[c].at[:, pl.ds(first - offsets[c], last - first)],
                            raw.at[:, pl.ds(first - lo, last - first)],
                            sem.at[len(copies)],
                        )
                    )
            for copy in copies:
                copy.start()
            for copy in copies:
                copy.wait()

    out_ref[...] = raw[...].T


def rows_of(place, pieces, rows):
    depth = pieces[0].shape[0]
    widths = tuple(x.shape[1] for x in pieces)
    return pl.pallas_call(
        functools.partial(rows_kernel, widths, rows),
        out_shape=jax.ShapeDtypeStruct((rows, depth), jnp.bfloat16),
        in_specs=[pl.BlockSpec(memory_space=pltpu.SMEM)]
        + [pl.BlockSpec(memory_space=pltpu.HBM)] * len(pieces),
        scratch_shapes=[
            pltpu.VMEM((depth, rows), jnp.bfloat16),
            pltpu.SemaphoreType.DMA((len(pieces),)),
        ],
        compiler_params=pltpu.CompilerParams(vmem_limit_bytes=VMEM_LIMIT),
        cost_estimate=pl.CostEstimate(flops=10**15, bytes_accessed=1, transcendentals=0),
    )(place, *pieces)


def gram_kernel(runs, tiles, starts, depth, scale, kept, added, *refs):
    lefts, refs = refs[:runs], refs[runs:]
    data, refs = refs[: runs * len(tiles)], list(refs[runs * len(tiles) :])
    old_ref = refs.pop(0) if added else None
    if kept:
        refs.pop(0)
    out_ref, left, b_buf, o_buf, left_sem, b_sem, o_sem = refs[:7]
    c_buf, c_sem = refs[7:] if added else (None, None)
    slots = b_buf.shape[0]

    def in_copies(i):
        slot = i % slots
        width = tiles[i][1]
        copies = [
            pltpu.make_async_copy(
                data[i * runs + run].at[:, pl.ds(starts[i * runs + run], width)],
                b_buf.at[slot, pl.ds(run * depth, depth), pl.ds(0, width)],
                b_sem.at[slot, run],
            )
            for run in range(runs)
        ]
        if added:
            copies.append(
                pltpu.make_async_copy(
                    old_ref.at[:, pl.ds(*tiles[i])],
                    c_buf.at[slot, :, pl.ds(0, width)],
                    c_sem.at[slot],
                )
            )
        return copies

    def out_copy(i):
        slot = i % slots
        return pltpu.make_async_copy(
            o_buf.at[slot, :, pl.ds(0, tiles[i][1])],
            out_ref.at[:, pl.ds(*tiles[i])],
            o_sem.at[slot],
        )

    left_copies = [
        pltpu.make_async_copy(
            lefts[run], left.at[:, pl.ds(run * depth, depth)], left_sem.at[run]
        )
        for run in range(runs)
    ]
    for copy in left_copies + in_copies(0):
        copy.start()
    for copy in left_copies:
        copy.wait()
    for i in range(1, min(slots - 1, len(tiles))):
        for copy in in_copies(i):
            copy.start()
    for i, (_, width) in enumerate(tiles):
        slot = i % slots
        if i + slots - 1 < len(tiles):
            for copy in in_copies(i + slots - 1):
                copy.start()
        for copy in in_copies(i):
            copy.wait()
        if i >= slots:
            out_copy(i - slots).wait()
        result = scale * jnp.dot(
            left[...], b_buf[slot, :, :width], preferred_element_type=jnp.float32
        )
        if added:
            result = result + c_buf[slot, :, :width].astype(jnp.float32)
        o_buf[slot, :, :width] = result.astype(o_buf.dtype)
        out_copy(i).start()
    for i in range(max(0, len(tiles) - slots), len(tiles)):
        out_copy(i).wait()


def gram(out, lefts, tiles, width, columns, scale, kind, old=None):
    runs = len(lefts)
    rows, depth = lefts[0].shape
    places = [(first, width) for first, _ in tiles]
    data = [x for _, arrays in tiles for x, _ in arrays]
    starts = [x for _, arrays in tiles for _, x in arrays]
    kept, added = out is not None, old is not None
    any_spec = pl.BlockSpec(memory_space=pltpu.HBM)
    operands = [*lefts, *data] + ([old] if added else []) + ([out] if kept else [])
    slots = min(4, len(tiles))
    scratch = [
        pltpu.VMEM((rows, runs * depth), jnp.bfloat16),
        pltpu.VMEM((slots, runs * depth, width), jnp.bfloat16),
        pltpu.VMEM((slots, rows, width), kind),
        pltpu.SemaphoreType.DMA((runs,)),
        pltpu.SemaphoreType.DMA((slots, runs)),
        pltpu.SemaphoreType.DMA((slots,)),
    ]
    if added:
        scratch += [pltpu.VMEM((slots, rows, width), old.dtype), pltpu.SemaphoreType.DMA((slots,))]
    total = sum(width for _, width in places)
    return pl.pallas_call(
        functools.partial(gram_kernel, runs, places, starts, depth, scale, kept, added),
        out_shape=jax.ShapeDtypeStruct((rows, columns), kind),
        in_specs=[any_spec] * len(operands),
        out_specs=any_spec,
        scratch_shapes=scratch,
        input_output_aliases={len(operands) - 1: 0} if kept else {},
        compiler_params=pltpu.CompilerParams(vmem_limit_bytes=VMEM_LIMIT),
        cost_estimate=pl.CostEstimate(flops=10**15, bytes_accessed=1, transcendentals=0),
    )(*operands)


def kv_of(keys, values, local_heads):
    group = HEADS // KV_HEADS
    kv_count = max(1, local_heads // group)
    kv_first = lax.axis_index("tensor") * local_heads // group
    own, prev = [], []
    for k in range(kv_count):
        parts = [lax.dynamic_slice_in_dim(x, (kv_first + k) * HD, HD, 1) for x in (keys, values)]
        own.append(jnp.concatenate(parts, 1))
        prev.append(shifted(own[k], "dp", 1))
    return list(zip(own, prev)), local_heads // kv_count


CHUNKS = 6


def per_device(queries, keys, values, page_start):
    tok_rows, slab = queries.shape
    local_heads = slab // HD
    runs = lax.axis_size("dp")
    kv, per_kv = kv_of(keys, values, local_heads)
    run_index = lax.axis_index("dp")
    start = (page_start - run_index * tok_rows).reshape(tok_rows, 1)
    place = run_index.reshape(1)
    rows = slab // runs
    scale = 2.0 / (tok_rows * runs)
    even = lax.axis_index("tensor") % 2 == 0

    size = local_heads // CHUNKS
    width = size * HD
    own, mirror, sibling = {}, {}, {}
    within = {}
    half = CHUNKS // 2
    last = runs - 1
    over_z = [("own", c, r) for r in range(1, runs) for c in range(CHUNKS)]
    over_z += [("mirror", c, last) for c in range(half, CHUNKS)]
    over_y = [(c, r) for r in range(last) for c in range(CHUNKS)]
    over_y += [(c, last) for c in range(half)]

    left = {}
    sums = {}
    steps = max(len(over_z), len(over_y))
    ended = {}
    swapped = []
    def tiles(kinds, chosen, some_runs):
        tables = (own, sibling, mirror)
        return [
            (
                k * slab + c * width,
                [(tables[k][c, r], within[c, r] if k == 1 else 0) for r in some_runs],
            )
            for c in chosen
            for k in kinds
        ]

    def rows_for(some_runs):
        for r in some_runs:
            if r not in left:
                left[r] = rows_of(place, [own[c, r] for c in range(CHUNKS)], rows)
        return [left[r] for r in some_runs]

    every = list(range(runs))
    everything = list(range(CHUNKS))
    first_runs, last_runs = every[: runs // 2], every[runs // 2 :]
    moved = (2, 1)
    done = last * CHUNKS
    work = {
        done - 12: [("rows", 0)],
        done - 11: [("rows", 1)],
        done - 10: [((0,), everything, first_runs, False)],
        done - 8: [(moved, [0, 1], first_runs, False)],
        done - 6: [(moved, [2, 3], first_runs, False)],
        done - 4: [(moved, [4, 5], first_runs, False)],
        done - 2: [("rows", 2)],
        done + 1: [("rows", 3)],
        done + 2: [((0,), everything, last_runs, True)],
        done + 3: [(moved, [0, half], last_runs, True)],
        done + 4: [(moved, [1, half + 1], last_runs, True)],
        done + 5: [(moved, [half - 1, CHUNKS - 1], last_runs, True)],
    }

    for step in range(steps + 3):
        before = ended.get(step - 2, [])
        if step < CHUNKS:
            first = step * size
            some = tie(start, *[prev for _, prev in kv]) if step == 1 else start
            own[step, 0] = attend(queries, *kv[first // per_kv], some, first, size)
        arrived = []
        if step < len(over_z):
            kind, c, r = over_z[step]
            table = own if kind == "own" else mirror
            value, sums = held(table[c, r - 1], sums, *before)
            table[c, r] = from_behind(value, "dp", 1)
            arrived.append(table[c, r])
        if step < len(over_y):
            c, r = over_y[step]
            value, sums = held(own[c, r], sums, *before)
            mirror[c, r] = over_tensor(value, 2)
            arrived.append(mirror[c, r])
        ended[step] = arrived
        past = step - 2
        swaps = []
        if 0 <= past < steps:
            swaps = [over_y[past]] + [x[1:] for x in over_z[past : past + 1] if x[0] == "mirror"]
        if swaps:
            pair = ([mirror[x] for x in swaps], [own[x] for x in swaps])
            pair, sums = held(pair, sums, *before, *swapped)
            sent = jnp.where(even, *[jnp.concatenate(x, 1) for x in pair])
            sent = over_tensor(sent, 1)
            swapped = [sent]
            sibling.update({x: sent for x in swaps})
            within.update({x: i * width for i, x in enumerate(swaps)})
        for job in work.pop(step, ()):
            if job[0] == "rows":
                ended[step] += rows_for([job[1]])
            else:
                kinds, chosen, some_runs, added = job
                lefts, pieces = rows_for(some_runs), tiles(kinds, chosen, some_runs)
                if added:
                    sums["all"] = gram(
                        sums.get("all"), lefts, pieces, width, 3 * slab, scale, jnp.float32, sums["half"]
                    )
                else:
                    sums["half"] = gram(
                        sums.get("half"), lefts, pieces, width, 3 * slab, scale, jnp.bfloat16
                    )
    assert not work
    return sums["all"]


def per_device_general(queries, keys, values, page_start):
    tok_rows, slab_width = queries.shape
    local_heads = slab_width // HD
    runs = lax.axis_size("dp")
    kv, per_kv = kv_of(keys, values, local_heads)
    run_index = lax.axis_index("dp")
    start = (page_start - run_index * tok_rows).reshape(tok_rows, 1)
    outputs = jnp.concatenate(
        [attend(queries, *kv[h // per_kv], start, h, per_kv) for h in range(0, local_heads, per_kv)], 1
    )
    steps = lax.axis_size("tensor") // 2 + 1
    rows = slab_width // runs
    moving = lax.all_gather(outputs, "dp", axis=0, tiled=True)
    left = lax.dynamic_slice_in_dim(moving, run_index * rows, rows, 1)
    tiles = []
    for offset in range(steps):
        if offset:
            moving = from_behind(moving, "tensor", -1)
        tiles.append(
            lax.dot_general(
                left, moving, (((0,), (0,)), ((), ())), preferred_element_type=jnp.float32
            )
        )
    return jnp.concatenate(tiles, 1) * (2.0 / (tok_rows * runs))


def solution(mesh):
    cores = mesh.shape["tensor"]
    rows = HEADS * HD // cores // mesh.shape["dp"]
    tuned = cores == 4 and rows % HD == 0
    return jax.shard_map(
        per_device if tuned else per_device_general,
        mesh=mesh,
        in_specs=(
            P(("groups", "dp"), "tensor"),
            P(("groups", "dp"), None),
            P(("groups", "dp"), None),
            P(("groups", "dp")),
        ),
        out_specs=P(("groups", "tensor", "dp"), None),
        check_vma=False,
    )
```

```python
import functools

import jax
import jax.numpy as jnp
from jax import lax
from jax.experimental import pallas as pl
from jax.experimental.pallas import tpu as pltpu
from jax.sharding import PartitionSpec as P

HEADS = 96
HD = 128
KV_HEADS = 8
PAGE = 512
TILE = 256
ROWS = 256
STEP = 2
LOG2E = 1.4426950408889634
VMEM_LIMIT = 56 * 1024 * 1024


def shifted(x, axis, by):
    devices = lax.axis_size(axis)
    pairs = [(i, i + by) for i in range(devices) if 0 <= i + by < devices]
    return lax.ppermute(x, axis, pairs)


def from_behind(value, axis, steps):
    count = lax.axis_size(axis)
    pairs = [(source, (source + steps) % count) for source in range(count)]
    return lax.ppermute(value, axis, pairs)


def over_tensor(value, bit):
    count = lax.axis_size("tensor")
    return lax.ppermute(value, "tensor", [(t, t ^ bit) for t in range(count)])


def tie(value, *after):
    return lax.optimization_barrier((value, *after))[0] if after else value


def held(value, sums, *after):
    return lax.optimization_barrier((value, sums, *after))[:2]


def attend_kernel(start_ref, q_ref, kp_ref, ko_ref, vp_ref, vo_ref, out_ref, bias_ref):
    rows = q_ref.shape[0]
    tiles = rows // TILE
    keys_seen = PAGE + TILE

    @pl.when(pl.program_id(0) == 0)
    def _():
        for tile in range(tiles):
            shape = (TILE, keys_seen)
            query = lax.broadcasted_iota(jnp.int32, shape, 0) + tile * TILE
            key = lax.broadcasted_iota(jnp.int32, shape, 1) + (tile * TILE - PAGE)
            first = start_ref[tile * TILE : (tile + 1) * TILE, :]
            visible = (key >= first) & (key <= query)
            bias_ref[tile] = jnp.where(visible, 0.0, -1e30)

    for tile in range(tiles):
        lo = tile * TILE
        key = jnp.concatenate([kp_ref[lo:, :], ko_ref[: lo + TILE, :]], 0)
        value = jnp.concatenate([vp_ref[lo:, :], vo_ref[: lo + TILE, :]], 0)
        value = jnp.concatenate([value, jnp.ones_like(value)], 1)
        for head in range(q_ref.shape[1] // HD):
            columns = slice(head * HD, (head + 1) * HD)
            scores = lax.dot_general(
                q_ref[lo : lo + TILE, columns],
                key,
                (((1,), (1,)), ((), ())),
                preferred_element_type=jnp.float32,
            )
            scores = scores + bias_ref[tile]
            top = jnp.max(scores, axis=-1, keepdims=True)
            expo = jnp.exp2((scores - top) * (LOG2E / HD**0.5)).astype(jnp.bfloat16)
            mixed = jnp.dot(expo, value, preferred_element_type=jnp.float32)
            out_ref[lo : lo + TILE, columns] = (mixed[:, :HD] / mixed[:, HD:]).astype(jnp.bfloat16)


def attend(queries, own_kv, prev_kv, start, first_head, heads):
    rows = queries.shape[0]
    step = STEP if heads % STEP == 0 and first_head % STEP == 0 else 1
    key_spec = pl.BlockSpec((PAGE, HD), lambda h: (0, 0))
    value_spec = pl.BlockSpec((PAGE, HD), lambda h: (0, 1))
    return pl.pallas_call(
        attend_kernel,
        grid=(heads // step,),
        out_shape=jax.ShapeDtypeStruct((rows, heads * HD), jnp.bfloat16),
        in_specs=[
            pl.BlockSpec((rows, 1), lambda h: (0, 0)),
            pl.BlockSpec((rows, step * HD), lambda h: (0, first_head // step + h)),
            key_spec,
            key_spec,
            value_spec,
            value_spec,
        ],
        out_specs=pl.BlockSpec((rows, step * HD), lambda h: (0, h)),
        scratch_shapes=[pltpu.VMEM((rows // TILE, TILE, PAGE + TILE), jnp.float32)],
        compiler_params=pltpu.CompilerParams(vmem_limit_bytes=VMEM_LIMIT),
        cost_estimate=pl.CostEstimate(flops=10**15, bytes_accessed=1, transcendentals=0),
    )(start, queries, prev_kv, own_kv, prev_kv, own_kv)


def rows_kernel(widths, rows, place_ref, *refs):
    chunks = len(widths)
    sources, (out_ref, raw, sem) = refs[:chunks], refs[chunks:]
    offsets = [sum(widths[:c]) for c in range(chunks)]
    for where in range(sum(widths) // rows):

        @pl.when(place_ref[0] == where)
        def _():
            lo, hi = where * rows, (where + 1) * rows
            copies = []
            for c in range(chunks):
                first, last = max(lo, offsets[c]), min(hi, offsets[c] + widths[c])
                if first < last:
                    copies.append(
                        pltpu.make_async_copy(
                            sources[c].at[:, pl.ds(first - offsets[c], last - first)],
                            raw.at[:, pl.ds(first - lo, last - first)],
                            sem.at[len(copies)],
                        )
                    )
            for copy in copies:
                copy.start()
            for copy in copies:
                copy.wait()

    out_ref[...] = raw[...].T


def rows_of(place, pieces, rows):
    depth = pieces[0].shape[0]
    widths = tuple(x.shape[1] for x in pieces)
    return pl.pallas_call(
        functools.partial(rows_kernel, widths, rows),
        out_shape=jax.ShapeDtypeStruct((rows, depth), jnp.bfloat16),
        in_specs=[pl.BlockSpec(memory_space=pltpu.SMEM)]
        + [pl.BlockSpec(memory_space=pltpu.HBM)] * len(pieces),
        scratch_shapes=[
            pltpu.VMEM((depth, rows), jnp.bfloat16),
            pltpu.SemaphoreType.DMA((len(pieces),)),
        ],
        compiler_params=pltpu.CompilerParams(vmem_limit_bytes=VMEM_LIMIT),
        cost_estimate=pl.CostEstimate(flops=10**15, bytes_accessed=1, transcendentals=0),
    )(place, *pieces)


def gram_kernel(runs, tiles, starts, depth, scale, kept, added, *refs):
    lefts, refs = refs[:runs], refs[runs:]
    data, refs = refs[: runs * len(tiles)], list(refs[runs * len(tiles) :])
    old_ref = refs.pop(0) if added else None
    if kept:
        refs.pop(0)
    out_ref, left, b_buf, o_buf, left_sem, b_sem, o_sem = refs[:7]
    c_buf, c_sem = refs[7:] if added else (None, None)
    slots = b_buf.shape[0]

    def in_copies(i):
        slot = i % slots
        width = tiles[i][1]
        copies = [
            pltpu.make_async_copy(
                data[i * runs + run].at[:, pl.ds(starts[i * runs + run], width)],
                b_buf.at[slot, pl.ds(run * depth, depth), pl.ds(0, width)],
                b_sem.at[slot, run],
            )
            for run in range(runs)
        ]
        if added:
            copies.append(
                pltpu.make_async_copy(
                    old_ref.at[:, pl.ds(*tiles[i])],
                    c_buf.at[slot, :, pl.ds(0, width)],
                    c_sem.at[slot],
                )
            )
        return copies

    def out_copy(i):
        slot = i % slots
        return pltpu.make_async_copy(
            o_buf.at[slot, :, pl.ds(0, tiles[i][1])],
            out_ref.at[:, pl.ds(*tiles[i])],
            o_sem.at[slot],
        )

    left_copies = [
        pltpu.make_async_copy(
            lefts[run], left.at[:, pl.ds(run * depth, depth)], left_sem.at[run]
        )
        for run in range(runs)
    ]
    for copy in left_copies + in_copies(0):
        copy.start()
    for copy in left_copies:
        copy.wait()
    for i in range(1, min(slots - 1, len(tiles))):
        for copy in in_copies(i):
            copy.start()
    for i, (_, width) in enumerate(tiles):
        slot = i % slots
        if i + slots - 1 < len(tiles):
            for copy in in_copies(i + slots - 1):
                copy.start()
        for copy in in_copies(i):
            copy.wait()
        if i >= slots:
            out_copy(i - slots).wait()

        def block(part, slot=slot, width=width):
            result = scale * jnp.dot(
                left[part, :], b_buf[slot, :, :width], preferred_element_type=jnp.float32
            )
            if added:
                result = result + c_buf[slot, part, :width].astype(jnp.float32)
            o_buf[slot, part, :width] = result.astype(o_buf.dtype)

        if added:
            block(slice(None))
        else:
            pl.loop(0, left.shape[0] // ROWS)(lambda n: block(pl.ds(pl.multiple_of(n * ROWS, ROWS), ROWS)))
        out_copy(i).start()
    for i in range(max(0, len(tiles) - slots), len(tiles)):
        out_copy(i).wait()


def gram(out, lefts, tiles, width, columns, scale, kind, old=None):
    runs = len(lefts)
    rows, depth = lefts[0].shape
    places = [(first, width) for first, _ in tiles]
    data = [x for _, arrays in tiles for x, _ in arrays]
    starts = [x for _, arrays in tiles for _, x in arrays]
    kept, added = out is not None, old is not None
    any_spec = pl.BlockSpec(memory_space=pltpu.HBM)
    operands = [*lefts, *data] + ([old] if added else []) + ([out] if kept else [])
    slots = min(4, len(tiles))
    scratch = [
        pltpu.VMEM((rows, runs * depth), jnp.bfloat16),
        pltpu.VMEM((slots, runs * depth, width), jnp.bfloat16),
        pltpu.VMEM((slots, rows, width), kind),
        pltpu.SemaphoreType.DMA((runs,)),
        pltpu.SemaphoreType.DMA((slots, runs)),
        pltpu.SemaphoreType.DMA((slots,)),
    ]
    if added:
        scratch += [pltpu.VMEM((slots, rows, width), old.dtype), pltpu.SemaphoreType.DMA((slots,))]
    total = sum(width for _, width in places)
    return pl.pallas_call(
        functools.partial(gram_kernel, runs, places, starts, depth, scale, kept, added),
        out_shape=jax.ShapeDtypeStruct((rows, columns), kind),
        in_specs=[any_spec] * len(operands),
        out_specs=any_spec,
        scratch_shapes=scratch,
        input_output_aliases={len(operands) - 1: 0} if kept else {},
        compiler_params=pltpu.CompilerParams(vmem_limit_bytes=VMEM_LIMIT),
        cost_estimate=pl.CostEstimate(flops=10**15, bytes_accessed=1, transcendentals=0),
    )(*operands)


def kv_of(keys, values, local_heads):
    group = HEADS // KV_HEADS
    kv_count = max(1, local_heads // group)
    kv_first = lax.axis_index("tensor") * local_heads // group
    own, prev = [], []
    for k in range(kv_count):
        parts = [lax.dynamic_slice_in_dim(x, (kv_first + k) * HD, HD, 1) for x in (keys, values)]
        own.append(jnp.concatenate(parts, 1))
        prev.append(shifted(own[k], "dp", 1))
    return list(zip(own, prev)), local_heads // kv_count


CHUNKS = 6


def per_device(queries, keys, values, page_start):
    tok_rows, slab = queries.shape
    local_heads = slab // HD
    runs = lax.axis_size("dp")
    kv, per_kv = kv_of(keys, values, local_heads)
    run_index = lax.axis_index("dp")
    start = (page_start - run_index * tok_rows).reshape(tok_rows, 1)
    place = run_index.reshape(1)
    rows = slab // runs
    scale = 2.0 / (tok_rows * runs)
    even = lax.axis_index("tensor") % 2 == 0

    size = local_heads // CHUNKS
    width = size * HD
    own, mirror, sibling = {}, {}, {}
    within = {}
    half = CHUNKS // 2
    last = runs - 1
    over_z = [("own", c, r) for r in range(1, runs) for c in range(CHUNKS)]
    over_z += [("mirror", c, last) for c in range(half, CHUNKS)]
    over_y = [(c, r) for r in range(last) for c in range(CHUNKS)]
    over_y += [(c, last) for c in range(half)]

    left = {}
    sums = {}
    steps = max(len(over_z), len(over_y))
    ended = {}
    swapped = []
    def tiles(kinds, chosen, some_runs):
        tables = (own, sibling, mirror)
        return [
            (
                k * slab + c * width,
                [(tables[k][c, r], within[c, r] if k == 1 else 0) for r in some_runs],
            )
            for c in chosen
            for k in kinds
        ]

    def rows_for(some_runs):
        for r in some_runs:
            if r not in left:
                left[r] = rows_of(place, [own[c, r] for c in range(CHUNKS)], rows)
        return [left[r] for r in some_runs]

    every = list(range(runs))
    everything = list(range(CHUNKS))
    first_runs, last_runs = every[: runs // 2], every[runs // 2 :]
    moved = (2, 1)
    done = last * CHUNKS
    work = {
        done - 12: [("rows", 0)],
        done - 11: [("rows", 1)],
        done - 10: [((0,), everything, first_runs, False)],
        done - 8: [(moved, [0, 1], first_runs, False)],
        done - 6: [(moved, [2, 3], first_runs, False)],
        done - 4: [(moved, [4, 5], first_runs, False)],
        done - 2: [("rows", 2)],
        done + 1: [("rows", 3)],
        done + 2: [((0,), everything, last_runs, True)],
        done + 3: [(moved, [0, half], last_runs, True)],
        done + 4: [(moved, [1, half + 1], last_runs, True)],
        done + 5: [(moved, [half - 1, CHUNKS - 1], last_runs, True)],
    }

    for step in range(steps + 3):
        before = ended.get(step - 2, [])
        if step < CHUNKS:
            first = step * size
            some = tie(start, *[prev for _, prev in kv]) if step == 1 else start
            own[step, 0] = attend(queries, *kv[first // per_kv], some, first, size)
        arrived = []
        if step < len(over_z):
            kind, c, r = over_z[step]
            table = own if kind == "own" else mirror
            value, sums = held(table[c, r - 1], sums, *before)
            table[c, r] = from_behind(value, "dp", 1)
            arrived.append(table[c, r])
        if step < len(over_y):
            c, r = over_y[step]
            value, sums = held(own[c, r], sums, *before)
            mirror[c, r] = over_tensor(value, 2)
            arrived.append(mirror[c, r])
        ended[step] = arrived
        past = step - 2
        swaps = []
        if 0 <= past < steps:
            swaps = [over_y[past]] + [x[1:] for x in over_z[past : past + 1] if x[0] == "mirror"]
        if swaps:
            pair = ([mirror[x] for x in swaps], [own[x] for x in swaps])
            pair, sums = held(pair, sums, *before, *swapped)
            sent = jnp.where(even, *[jnp.concatenate(x, 1) for x in pair])
            sent = over_tensor(sent, 1)
            swapped = [sent]
            sibling.update({x: sent for x in swaps})
            within.update({x: i * width for i, x in enumerate(swaps)})
        for job in work.pop(step, ()):
            if job[0] == "rows":
                ended[step] += rows_for([job[1]])
            else:
                kinds, chosen, some_runs, added = job
                lefts, pieces = rows_for(some_runs), tiles(kinds, chosen, some_runs)
                if added:
                    sums["all"] = gram(
                        sums.get("all"), lefts, pieces, width, 3 * slab, scale, jnp.float32, sums["half"]
                    )
                else:
                    sums["half"] = gram(
                        sums.get("half"), lefts, pieces, width, 3 * slab, scale, jnp.bfloat16
                    )
    assert not work
    return sums["all"]


def per_device_general(queries, keys, values, page_start):
    tok_rows, slab_width = queries.shape
    local_heads = slab_width // HD
    runs = lax.axis_size("dp")
    kv, per_kv = kv_of(keys, values, local_heads)
    run_index = lax.axis_index("dp")
    start = (page_start - run_index * tok_rows).reshape(tok_rows, 1)
    outputs = jnp.concatenate(
        [attend(queries, *kv[h // per_kv], start, h, per_kv) for h in range(0, local_heads, per_kv)], 1
    )
    steps = lax.axis_size("tensor") // 2 + 1
    rows = slab_width // runs
    moving = lax.all_gather(outputs, "dp", axis=0, tiled=True)
    left = lax.dynamic_slice_in_dim(moving, run_index * rows, rows, 1)
    tiles = []
    for offset in range(steps):
        if offset:
            moving = from_behind(moving, "tensor", -1)
        tiles.append(
            lax.dot_general(
                left, moving, (((0,), (0,)), ((), ())), preferred_element_type=jnp.float32
            )
        )
    return jnp.concatenate(tiles, 1) * (2.0 / (tok_rows * runs))


def solution(mesh):
    cores = mesh.shape["tensor"]
    rows = HEADS * HD // cores // mesh.shape["dp"]
    tuned = cores == 4 and rows % HD == 0
    return jax.shard_map(
        per_device if tuned else per_device_general,
        mesh=mesh,
        in_specs=(
            P(("groups", "dp"), "tensor"),
            P(("groups", "dp"), None),
            P(("groups", "dp"), None),
            P(("groups", "dp")),
        ),
        out_specs=P(("groups", "tensor", "dp"), None),
        check_vma=False,
    )
```

```python
import functools

import jax
import jax.numpy as jnp
from jax import lax
from jax.experimental import pallas as pl
from jax.experimental.pallas import tpu as pltpu
from jax.sharding import PartitionSpec as P

HEADS = 96
HD = 128
KV_HEADS = 8
PAGE = 512
TILE = 256
ROWS = 256
STEP = 2
LOG2E = 1.4426950408889634
VMEM_LIMIT = 56 * 1024 * 1024


def shifted(x, axis, by):
    devices = lax.axis_size(axis)
    pairs = [(i, i + by) for i in range(devices) if 0 <= i + by < devices]
    return lax.ppermute(x, axis, pairs)


def from_behind(value, axis, steps):
    count = lax.axis_size(axis)
    pairs = [(source, (source + steps) % count) for source in range(count)]
    return lax.ppermute(value, axis, pairs)


def over_tensor(value, bit):
    count = lax.axis_size("tensor")
    return lax.ppermute(value, "tensor", [(t, t ^ bit) for t in range(count)])


def tie(value, *after):
    return lax.optimization_barrier((value, *after))[0] if after else value


def held(value, sums, *after):
    return lax.optimization_barrier((value, sums, *after))[:2]


def attend_kernel(start_ref, q_ref, kp_ref, ko_ref, vp_ref, vo_ref, out_ref, bias_ref):
    rows = q_ref.shape[0]
    tiles = rows // TILE
    keys_seen = PAGE + TILE

    @pl.when(pl.program_id(0) == 0)
    def _():
        for tile in range(tiles):
            shape = (TILE, keys_seen)
            query = lax.broadcasted_iota(jnp.int32, shape, 0) + tile * TILE
            key = lax.broadcasted_iota(jnp.int32, shape, 1) + (tile * TILE - PAGE)
            first = start_ref[tile * TILE : (tile + 1) * TILE, :]
            visible = (key >= first) & (key <= query)
            bias_ref[tile] = jnp.where(visible, 0.0, -1e30)

    for tile in range(tiles):
        lo = tile * TILE
        key = jnp.concatenate([kp_ref[lo:, :], ko_ref[: lo + TILE, :]], 0)
        value = jnp.concatenate([vp_ref[lo:, :], vo_ref[: lo + TILE, :]], 0)
        value = jnp.concatenate([value, jnp.ones_like(value)], 1)
        for head in range(q_ref.shape[1] // HD):
            columns = slice(head * HD, (head + 1) * HD)
            scores = lax.dot_general(
                q_ref[lo : lo + TILE, columns],
                key,
                (((1,), (1,)), ((), ())),
                preferred_element_type=jnp.float32,
            )
            scores = scores + bias_ref[tile]
            top = jnp.max(scores, axis=-1, keepdims=True)
            expo = jnp.exp2((scores - top) * (LOG2E / HD**0.5)).astype(jnp.bfloat16)
            mixed = jnp.dot(expo, value, preferred_element_type=jnp.float32)
            out_ref[lo : lo + TILE, columns] = (mixed[:, :HD] / mixed[:, HD:]).astype(jnp.bfloat16)


def attend(queries, own_kv, prev_kv, start, first_head, heads):
    rows = queries.shape[0]
    step = STEP if heads % STEP == 0 and first_head % STEP == 0 else 1
    key_spec = pl.BlockSpec((PAGE, HD), lambda h: (0, 0))
    value_spec = pl.BlockSpec((PAGE, HD), lambda h: (0, 1))
    return pl.pallas_call(
        attend_kernel,
        grid=(heads // step,),
        out_shape=jax.ShapeDtypeStruct((rows, heads * HD), jnp.bfloat16),
        in_specs=[
            pl.BlockSpec((rows, 1), lambda h: (0, 0)),
            pl.BlockSpec((rows, step * HD), lambda h: (0, first_head // step + h)),
            key_spec,
            key_spec,
            value_spec,
            value_spec,
        ],
        out_specs=pl.BlockSpec((rows, step * HD), lambda h: (0, h)),
        scratch_shapes=[pltpu.VMEM((rows // TILE, TILE, PAGE + TILE), jnp.float32)],
        compiler_params=pltpu.CompilerParams(vmem_limit_bytes=VMEM_LIMIT),
        cost_estimate=pl.CostEstimate(flops=10**15, bytes_accessed=1, transcendentals=0),
    )(start, queries, prev_kv, own_kv, prev_kv, own_kv)


def rows_kernel(widths, rows, place_ref, *refs):
    chunks = len(widths)
    sources, (out_ref, raw, sem) = refs[:chunks], refs[chunks:]
    offsets = [sum(widths[:c]) for c in range(chunks)]
    for where in range(sum(widths) // rows):

        @pl.when(place_ref[0] == where)
        def _():
            lo, hi = where * rows, (where + 1) * rows
            copies = []
            for c in range(chunks):
                first, last = max(lo, offsets[c]), min(hi, offsets[c] + widths[c])
                if first < last:
                    copies.append(
                        pltpu.make_async_copy(
                            sources[c].at[:, pl.ds(first - offsets[c], last - first)],
                            raw.at[:, pl.ds(first - lo, last - first)],
                            sem.at[len(copies)],
                        )
                    )
            for copy in copies:
                copy.start()
            for copy in copies:
                copy.wait()

    out_ref[...] = raw[...].T


def rows_of(place, pieces, rows):
    depth = pieces[0].shape[0]
    widths = tuple(x.shape[1] for x in pieces)
    return pl.pallas_call(
        functools.partial(rows_kernel, widths, rows),
        out_shape=jax.ShapeDtypeStruct((rows, depth), jnp.bfloat16),
        in_specs=[pl.BlockSpec(memory_space=pltpu.SMEM)]
        + [pl.BlockSpec(memory_space=pltpu.HBM)] * len(pieces),
        scratch_shapes=[
            pltpu.VMEM((depth, rows), jnp.bfloat16),
            pltpu.SemaphoreType.DMA((len(pieces),)),
        ],
        compiler_params=pltpu.CompilerParams(vmem_limit_bytes=VMEM_LIMIT),
        cost_estimate=pl.CostEstimate(flops=10**15, bytes_accessed=1, transcendentals=0),
    )(place, *pieces)


def gram_kernel(runs, tiles, counts, starts, depth, scale, kept, added, in_place, *refs):
    lefts, refs = refs[:runs], refs[runs:]
    data, refs = refs[: len(starts)], list(refs[len(starts) :])
    old_ref = refs.pop(0) if added else None
    if kept and not in_place:
        refs.pop(0)
    out_ref, left, b_buf, o_buf, left_sem, b_sem, o_sem = refs[:7]
    c_buf, c_sem = refs[7:] if added else (None, None)
    slots = b_buf.shape[0]

    def in_copies(i):
        slot = i % slots
        width = tiles[i][1]
        copies = [
            pltpu.make_async_copy(
                data[n].at[:, pl.ds(starts[n], width)],
                b_buf.at[slot, pl.ds(run * depth, depth), pl.ds(0, width)],
                b_sem.at[slot, run],
            )
            for run, n in zip(range(runs - counts[i], runs), range(sum(counts[:i]), sum(counts)))
        ]
        if added:
            copies.append(
                pltpu.make_async_copy(
                    old_ref.at[:, pl.ds(*tiles[i])],
                    c_buf.at[slot, :, pl.ds(0, width)],
                    c_sem.at[slot],
                )
            )
        return copies

    def out_copy(i):
        slot = i % slots
        return pltpu.make_async_copy(
            o_buf.at[slot, :, pl.ds(0, tiles[i][1])],
            out_ref.at[:, pl.ds(*tiles[i])],
            o_sem.at[slot],
        )

    left_copies = [
        pltpu.make_async_copy(
            lefts[run], left.at[:, pl.ds(run * depth, depth)], left_sem.at[run]
        )
        for run in range(runs)
    ]
    for copy in left_copies + in_copies(0):
        copy.start()
    for copy in left_copies:
        copy.wait()
    for i in range(1, min(slots - 1, len(tiles))):
        for copy in in_copies(i):
            copy.start()
    for i, (_, width) in enumerate(tiles):
        slot = i % slots
        if i + slots - 1 < len(tiles):
            for copy in in_copies(i + slots - 1):
                copy.start()
        for copy in in_copies(i):
            copy.wait()
        if i >= slots:
            out_copy(i - slots).wait()

        def block(part, slot=slot, width=width, seen=slice((runs - counts[i]) * depth, None)):
            result = scale * jnp.dot(
                left[part, seen], b_buf[slot, seen, :width], preferred_element_type=jnp.float32
            )
            if added:
                result = result + c_buf[slot, part, :width].astype(jnp.float32)
            o_buf[slot, part, :width] = result.astype(o_buf.dtype)

        if added and not in_place:
            block(slice(None))
        else:
            pl.loop(0, left.shape[0] // ROWS)(lambda n: block(pl.ds(pl.multiple_of(n * ROWS, ROWS), ROWS)))
        out_copy(i).start()
    for i in range(max(0, len(tiles) - slots), len(tiles)):
        out_copy(i).wait()


def gram(out, lefts, tiles, width, columns, scale, kind, old=None, add=False):
    runs = len(lefts)
    rows, depth = lefts[0].shape
    places = [(first, width) for first, _ in tiles]
    data = [x for _, arrays in tiles for x, _ in arrays]
    starts = [x for _, arrays in tiles for _, x in arrays]
    counts = [len(arrays) for _, arrays in tiles]
    kept, added = out is not None, add or old is not None
    any_spec = pl.BlockSpec(memory_space=pltpu.HBM)
    operands = [*lefts, *data] + ([] if old is None else [old]) + ([out] if kept else [])
    slots = min(4, len(tiles))
    scratch = [
        pltpu.VMEM((rows, runs * depth), jnp.bfloat16),
        pltpu.VMEM((slots, runs * depth, width), jnp.bfloat16),
        pltpu.VMEM((slots, rows, width), kind),
        pltpu.SemaphoreType.DMA((runs,)),
        pltpu.SemaphoreType.DMA((slots, runs)),
        pltpu.SemaphoreType.DMA((slots,)),
    ]
    if added:
        scratch += [pltpu.VMEM((slots, rows, width), out.dtype if old is None else old.dtype), pltpu.SemaphoreType.DMA((slots,))]
    total = sum(width for _, width in places)
    return pl.pallas_call(
        functools.partial(gram_kernel, runs, places, counts, starts, depth, scale, kept, added, add),
        out_shape=jax.ShapeDtypeStruct((rows, columns), kind),
        in_specs=[any_spec] * len(operands),
        out_specs=any_spec,
        scratch_shapes=scratch,
        input_output_aliases={len(operands) - 1: 0} if kept else {},
        compiler_params=pltpu.CompilerParams(vmem_limit_bytes=VMEM_LIMIT),
        cost_estimate=pl.CostEstimate(flops=10**15, bytes_accessed=1, transcendentals=0),
    )(*operands)


def kv_of(keys, values, local_heads):
    group = HEADS // KV_HEADS
    kv_count = max(1, local_heads // group)
    kv_first = lax.axis_index("tensor") * local_heads // group
    own, prev = [], []
    for k in range(kv_count):
        parts = [lax.dynamic_slice_in_dim(x, (kv_first + k) * HD, HD, 1) for x in (keys, values)]
        own.append(jnp.concatenate(parts, 1))
        prev.append(shifted(own[k], "dp", 1))
    return list(zip(own, prev)), local_heads // kv_count


CHUNKS = 6


def per_device(queries, keys, values, page_start):
    tok_rows, slab = queries.shape
    local_heads = slab // HD
    runs = lax.axis_size("dp")
    kv, per_kv = kv_of(keys, values, local_heads)
    run_index = lax.axis_index("dp")
    start = (page_start - run_index * tok_rows).reshape(tok_rows, 1)
    place = run_index.reshape(1)
    rows = slab // runs
    scale = 2.0 / (tok_rows * runs)
    even = lax.axis_index("tensor") % 2 == 0

    size = local_heads // CHUNKS
    width = size * HD
    own, mirror, sibling = {}, {}, {}
    within = {}
    half = CHUNKS // 2
    last = runs - 1
    over_z = [("own", c, r) for r in range(1, runs) for c in range(CHUNKS)]
    over_z += [("mirror", c, last) for c in range(half, CHUNKS)]
    over_y = [(c, r) for r in range(last) for c in range(CHUNKS)]
    over_y += [(c, last) for c in range(half)]

    left = {}
    sums = {}
    steps = max(len(over_z), len(over_y))
    ended = {}
    swapped = []
    def tiles(kinds, chosen, some_runs):
        tables = (own, sibling, mirror)
        return [
            (
                k * slab + c * width,
                [
                    (tables[k][c, r], within[c, r] if k == 1 else 0)
                    for r in some_runs
                    if (k, c, r) not in added
                ],
            )
            for c in chosen
            for k in kinds
        ]

    def rows_for(some_runs):
        for r in some_runs:
            if r not in left:
                left[r] = rows_of(place, [own[c, r] for c in range(CHUNKS)], rows)
        return [left[r] for r in some_runs]

    every = list(range(runs))
    everything = list(range(CHUNKS))
    moved = (2, 1)
    done = last * CHUNKS
    work = {
        done - 12: [("rows", 0)],
        done - 11: [("rows", 1)],
        done - 10: [((0,), everything[:half], [0, 1], False)],
        done - 9: [((0,), everything[half:], [0, 1], False)],
        done - 8: [(moved, [0, 1], [0, 1], False)],
        done - 6: [(moved, [2, 3], [0, 1], False)],
        done - 5: [("rows", 2)],
        done - 4: [(moved, [4, 5], [0, 1], False)],
        done - 3: [((0,), everything, [2], False)],
        done - 2: [(moved, [0, 1], [2], False)],
        done: [(moved, [2, 3], [2], False)],
        done + 1: [("rows", 3)],
        done + 2: [((0,), everything, [3], True)],
        done + 3: [(moved, [0, half], [3], True)],
        done + 4: [(moved, [1, half + 1], [2, 3], True)],
        done + 5: [(moved, [half - 1, CHUNKS - 1], [2, 3], True)],
    }
    added = set()

    for step in range(steps + 3):
        before = ended.get(step - 2, [])
        if step < CHUNKS:
            first = step * size
            some = tie(start, *[prev for _, prev in kv]) if step == 1 else start
            own[step, 0] = attend(queries, *kv[first // per_kv], some, first, size)
        arrived = []
        if step < len(over_z):
            kind, c, r = over_z[step]
            table = own if kind == "own" else mirror
            value, sums = held(table[c, r - 1], sums, *before)
            table[c, r] = from_behind(value, "dp", 1)
            arrived.append(table[c, r])
        if step < len(over_y):
            c, r = over_y[step]
            value, sums = held(own[c, r], sums, *before)
            mirror[c, r] = over_tensor(value, 2)
            arrived.append(mirror[c, r])
        ended[step] = arrived
        past = step - 2
        swaps = []
        if 0 <= past < steps:
            swaps = [over_y[past]] + [x[1:] for x in over_z[past : past + 1] if x[0] == "mirror"]
        if swaps:
            pair = ([mirror[x] for x in swaps], [own[x] for x in swaps])
            pair, sums = held(pair, sums, *before, *swapped)
            sent = jnp.where(even, *[jnp.concatenate(x, 1) for x in pair])
            sent = over_tensor(sent, 1)
            swapped = [sent]
            sibling.update({x: sent for x in swaps})
            within.update({x: i * width for i, x in enumerate(swaps)})
        for job in work.pop(step, ()):
            if job[0] == "rows":
                ended[step] += rows_for([job[1]])
            else:
                kinds, chosen, some_runs, final = job
                lefts, pieces = rows_for(some_runs), tiles(kinds, chosen, some_runs)
                added.update((k, c, r) for k in kinds for c in chosen for r in some_runs)
                args = (lefts, pieces, width, 3 * slab, scale)
                if final:
                    sums["all"] = gram(sums.get("all"), *args, jnp.float32, sums["half"])
                else:
                    sums["half"] = gram(sums.get("half"), *args, jnp.bfloat16, add=some_runs[0] > 0)
    assert not work and len(added) == 3 * CHUNKS * runs
    return sums["all"]


def per_device_general(queries, keys, values, page_start):
    tok_rows, slab_width = queries.shape
    local_heads = slab_width // HD
    runs = lax.axis_size("dp")
    kv, per_kv = kv_of(keys, values, local_heads)
    run_index = lax.axis_index("dp")
    start = (page_start - run_index * tok_rows).reshape(tok_rows, 1)
    outputs = jnp.concatenate(
        [attend(queries, *kv[h // per_kv], start, h, per_kv) for h in range(0, local_heads, per_kv)], 1
    )
    steps = lax.axis_size("tensor") // 2 + 1
    rows = slab_width // runs
    moving = lax.all_gather(outputs, "dp", axis=0, tiled=True)
    left = lax.dynamic_slice_in_dim(moving, run_index * rows, rows, 1)
    tiles = []
    for offset in range(steps):
        if offset:
            moving = from_behind(moving, "tensor", -1)
        tiles.append(
            lax.dot_general(
                left, moving, (((0,), (0,)), ((), ())), preferred_element_type=jnp.float32
            )
        )
    return jnp.concatenate(tiles, 1) * (2.0 / (tok_rows * runs))


def solution(mesh):
    cores = mesh.shape["tensor"]
    rows = HEADS * HD // cores // mesh.shape["dp"]
    tuned = cores == 4 and rows % HD == 0
    return jax.shard_map(
        per_device if tuned else per_device_general,
        mesh=mesh,
        in_specs=(
            P(("groups", "dp"), "tensor"),
            P(("groups", "dp"), None),
            P(("groups", "dp"), None),
            P(("groups", "dp")),
        ),
        out_specs=P(("groups", "tensor", "dp"), None),
        check_vma=False,
    )
```

```python
import functools

import jax
import jax.numpy as jnp
from jax import lax
from jax.experimental import pallas as pl
from jax.experimental.pallas import tpu as pltpu
from jax.sharding import PartitionSpec as P

HEADS = 96
HD = 128
KV_HEADS = 8
PAGE = 512
TILE = 256
ROWS = 256
STEP = 2
LOG2E = 1.4426950408889634
VMEM_LIMIT = 56 * 1024 * 1024


def shifted(x, axis, by):
    devices = lax.axis_size(axis)
    pairs = [(i, i + by) for i in range(devices) if 0 <= i + by < devices]
    return lax.ppermute(x, axis, pairs)


def from_behind(value, axis, steps):
    count = lax.axis_size(axis)
    pairs = [(source, (source + steps) % count) for source in range(count)]
    return lax.ppermute(value, axis, pairs)


def over_tensor(value, bit):
    count = lax.axis_size("tensor")
    return lax.ppermute(value, "tensor", [(t, t ^ bit) for t in range(count)])


def tie(value, *after):
    return lax.optimization_barrier((value, *after))[0] if after else value


def held(value, sums, *after):
    return lax.optimization_barrier((value, sums, *after))[:2]


def attend_kernel(start_ref, q_ref, kp_ref, ko_ref, vp_ref, vo_ref, out_ref, bias_ref):
    rows = q_ref.shape[0]
    tiles = rows // TILE
    keys_seen = PAGE + TILE

    @pl.when(pl.program_id(0) == 0)
    def _():
        for tile in range(tiles):
            shape = (TILE, keys_seen)
            query = lax.broadcasted_iota(jnp.int32, shape, 0) + tile * TILE
            key = lax.broadcasted_iota(jnp.int32, shape, 1) + (tile * TILE - PAGE)
            first = start_ref[tile * TILE : (tile + 1) * TILE, :]
            visible = (key >= first) & (key <= query)
            bias_ref[tile] = jnp.where(visible, 0.0, -1e30)

    for tile in range(tiles):
        lo = tile * TILE
        key = jnp.concatenate([kp_ref[lo:, :], ko_ref[: lo + TILE, :]], 0)
        value = jnp.concatenate([vp_ref[lo:, :], vo_ref[: lo + TILE, :]], 0)
        value = jnp.concatenate([value, jnp.ones_like(value)], 1)
        for head in range(q_ref.shape[1] // HD):
            columns = slice(head * HD, (head + 1) * HD)
            scores = lax.dot_general(
                q_ref[lo : lo + TILE, columns],
                key,
                (((1,), (1,)), ((), ())),
                preferred_element_type=jnp.float32,
            )
            scores = scores + bias_ref[tile]
            top = jnp.max(scores, axis=-1, keepdims=True)
            expo = jnp.exp2((scores - top) * (LOG2E / HD**0.5)).astype(jnp.bfloat16)
            mixed = jnp.dot(expo, value, preferred_element_type=jnp.float32)
            out_ref[lo : lo + TILE, columns] = (mixed[:, :HD] / mixed[:, HD:]).astype(jnp.bfloat16)


def attend(queries, own_kv, prev_kv, start, first_head, heads):
    rows = queries.shape[0]
    step = heads if first_head == 0 and heads <= 2 * STEP else STEP
    step = step if heads % step == 0 and first_head % step == 0 else 1
    key_spec = pl.BlockSpec((PAGE, HD), lambda h: (0, 0))
    value_spec = pl.BlockSpec((PAGE, HD), lambda h: (0, 1))
    return pl.pallas_call(
        attend_kernel,
        grid=(heads // step,),
        out_shape=jax.ShapeDtypeStruct((rows, heads * HD), jnp.bfloat16),
        in_specs=[
            pl.BlockSpec((rows, 1), lambda h: (0, 0)),
            pl.BlockSpec((rows, step * HD), lambda h: (0, first_head // step + h)),
            key_spec,
            key_spec,
            value_spec,
            value_spec,
        ],
        out_specs=pl.BlockSpec((rows, step * HD), lambda h: (0, h)),
        scratch_shapes=[pltpu.VMEM((rows // TILE, TILE, PAGE + TILE), jnp.float32)],
        compiler_params=pltpu.CompilerParams(vmem_limit_bytes=VMEM_LIMIT),
        cost_estimate=pl.CostEstimate(flops=10**15, bytes_accessed=1, transcendentals=0),
    )(start, queries, prev_kv, own_kv, prev_kv, own_kv)


def rows_kernel(widths, rows, place_ref, *refs):
    chunks = len(widths)
    sources, (out_ref, raw, sem) = refs[:chunks], refs[chunks:]
    offsets = [sum(widths[:c]) for c in range(chunks)]
    for where in range(sum(widths) // rows):

        @pl.when(place_ref[0] == where)
        def _():
            lo, hi = where * rows, (where + 1) * rows
            copies = []
            for c in range(chunks):
                first, last = max(lo, offsets[c]), min(hi, offsets[c] + widths[c])
                if first < last:
                    copies.append(
                        pltpu.make_async_copy(
                            sources[c].at[:, pl.ds(first - offsets[c], last - first)],
                            raw.at[:, pl.ds(first - lo, last - first)],
                            sem.at[len(copies)],
                        )
                    )
            for copy in copies:
                copy.start()
            for copy in copies:
                copy.wait()

    out_ref[...] = raw[...].T


def rows_of(place, pieces, rows):
    depth = pieces[0].shape[0]
    widths = tuple(x.shape[1] for x in pieces)
    return pl.pallas_call(
        functools.partial(rows_kernel, widths, rows),
        out_shape=jax.ShapeDtypeStruct((rows, depth), jnp.bfloat16),
        in_specs=[pl.BlockSpec(memory_space=pltpu.SMEM)]
        + [pl.BlockSpec(memory_space=pltpu.HBM)] * len(pieces),
        scratch_shapes=[
            pltpu.VMEM((depth, rows), jnp.bfloat16),
            pltpu.SemaphoreType.DMA((len(pieces),)),
        ],
        compiler_params=pltpu.CompilerParams(vmem_limit_bytes=VMEM_LIMIT),
        cost_estimate=pl.CostEstimate(flops=10**15, bytes_accessed=1, transcendentals=0),
    )(place, *pieces)


def gram_kernel(runs, tiles, counts, starts, depth, scale, kept, added, in_place, *refs):
    lefts, refs = refs[:runs], refs[runs:]
    data, refs = refs[: len(starts)], list(refs[len(starts) :])
    old_ref = refs.pop(0) if added else None
    if kept and not in_place:
        refs.pop(0)
    out_ref, left, b_buf, o_buf, left_sem, b_sem, o_sem = refs[:7]
    c_buf, c_sem = refs[7:] if added else (None, None)
    slots = b_buf.shape[0]

    def in_copies(i):
        slot = i % slots
        width = tiles[i][1]
        copies = [
            pltpu.make_async_copy(
                data[n].at[:, pl.ds(starts[n], width)],
                b_buf.at[slot, pl.ds(run * depth, depth), pl.ds(0, width)],
                b_sem.at[slot, run],
            )
            for run, n in zip(range(runs - counts[i], runs), range(sum(counts[:i]), sum(counts)))
        ]
        if added:
            copies.append(
                pltpu.make_async_copy(
                    old_ref.at[:, pl.ds(*tiles[i])],
                    c_buf.at[slot, :, pl.ds(0, width)],
                    c_sem.at[slot],
                )
            )
        return copies

    def out_copy(i):
        slot = i % slots
        return pltpu.make_async_copy(
            o_buf.at[slot, :, pl.ds(0, tiles[i][1])],
            out_ref.at[:, pl.ds(*tiles[i])],
            o_sem.at[slot],
        )

    left_copies = [
        pltpu.make_async_copy(
            lefts[run], left.at[:, pl.ds(run * depth, depth)], left_sem.at[run]
        )
        for run in range(runs)
    ]
    for copy in left_copies + in_copies(0):
        copy.start()
    for copy in left_copies:
        copy.wait()
    for i in range(1, min(slots - 1, len(tiles))):
        for copy in in_copies(i):
            copy.start()
    for i, (_, width) in enumerate(tiles):
        slot = i % slots
        if i + slots - 1 < len(tiles):
            for copy in in_copies(i + slots - 1):
                copy.start()
        for copy in in_copies(i):
            copy.wait()
        if i >= slots:
            out_copy(i - slots).wait()

        def block(part, slot=slot, width=width, seen=slice((runs - counts[i]) * depth, None)):
            result = scale * jnp.dot(
                left[part, seen], b_buf[slot, seen, :width], preferred_element_type=jnp.float32
            )
            if added:
                result = result + c_buf[slot, part, :width].astype(jnp.float32)
            o_buf[slot, part, :width] = result.astype(o_buf.dtype)

        if added and not in_place:
            block(slice(None))
        else:
            pl.loop(0, left.shape[0] // ROWS)(lambda n: block(pl.ds(pl.multiple_of(n * ROWS, ROWS), ROWS)))
        out_copy(i).start()
    for i in range(max(0, len(tiles) - slots), len(tiles)):
        out_copy(i).wait()


def gram(out, lefts, tiles, width, columns, scale, kind, old=None, add=False):
    runs = len(lefts)
    rows, depth = lefts[0].shape
    places = [(first, width) for first, _ in tiles]
    data = [x for _, arrays in tiles for x, _ in arrays]
    starts = [x for _, arrays in tiles for _, x in arrays]
    counts = [len(arrays) for _, arrays in tiles]
    kept, added = out is not None, add or old is not None
    any_spec = pl.BlockSpec(memory_space=pltpu.HBM)
    operands = [*lefts, *data] + ([] if old is None else [old]) + ([out] if kept else [])
    slots = min(4, len(tiles))
    scratch = [
        pltpu.VMEM((rows, runs * depth), jnp.bfloat16),
        pltpu.VMEM((slots, runs * depth, width), jnp.bfloat16),
        pltpu.VMEM((slots, rows, width), kind),
        pltpu.SemaphoreType.DMA((runs,)),
        pltpu.SemaphoreType.DMA((slots, runs)),
        pltpu.SemaphoreType.DMA((slots,)),
    ]
    if added:
        scratch += [pltpu.VMEM((slots, rows, width), out.dtype if old is None else old.dtype), pltpu.SemaphoreType.DMA((slots,))]
    total = sum(width for _, width in places)
    return pl.pallas_call(
        functools.partial(gram_kernel, runs, places, counts, starts, depth, scale, kept, added, add),
        out_shape=jax.ShapeDtypeStruct((rows, columns), kind),
        in_specs=[any_spec] * len(operands),
        out_specs=any_spec,
        scratch_shapes=scratch,
        input_output_aliases={len(operands) - 1: 0} if kept else {},
        compiler_params=pltpu.CompilerParams(vmem_limit_bytes=VMEM_LIMIT),
        cost_estimate=pl.CostEstimate(flops=10**15, bytes_accessed=1, transcendentals=0),
    )(*operands)


def kv_of(keys, values, local_heads):
    group = HEADS // KV_HEADS
    kv_count = max(1, local_heads // group)
    kv_first = lax.axis_index("tensor") * local_heads // group
    own, prev = [], []
    for k in range(kv_count):
        parts = [lax.dynamic_slice_in_dim(x, (kv_first + k) * HD, HD, 1) for x in (keys, values)]
        own.append(jnp.concatenate(parts, 1))
        prev.append(shifted(own[k], "dp", 1))
    return list(zip(own, prev)), local_heads // kv_count


CHUNKS = 6


def per_device(queries, keys, values, page_start):
    tok_rows, slab = queries.shape
    local_heads = slab // HD
    runs = lax.axis_size("dp")
    kv, per_kv = kv_of(keys, values, local_heads)
    run_index = lax.axis_index("dp")
    start = (page_start - run_index * tok_rows).reshape(tok_rows, 1)
    place = run_index.reshape(1)
    rows = slab // runs
    scale = 2.0 / (tok_rows * runs)
    even = lax.axis_index("tensor") % 2 == 0

    size = local_heads // CHUNKS
    width = size * HD
    own, mirror, sibling = {}, {}, {}
    within = {}
    half = CHUNKS // 2
    last = runs - 1
    over_z = [("own", c, r) for r in range(1, runs) for c in range(CHUNKS)]
    over_z += [("mirror", c, last) for c in range(half, CHUNKS)]
    over_y = [(c, r) for r in range(last) for c in range(CHUNKS)]
    over_y += [(c, last) for c in range(half)]

    left = {}
    sums = {}
    steps = max(len(over_z), len(over_y))
    ended = {}
    swapped = []
    def tiles(kinds, chosen, some_runs):
        tables = (own, sibling, mirror)
        return [
            (
                k * slab + c * width,
                [
                    (tables[k][c, r], within[c, r] if k == 1 else 0)
                    for r in some_runs
                    if (k, c, r) not in added
                ],
            )
            for c in chosen
            for k in kinds
        ]

    def rows_for(some_runs):
        for r in some_runs:
            if r not in left:
                left[r] = rows_of(place, [own[c, r] for c in range(CHUNKS)], rows)
        return [left[r] for r in some_runs]

    every = list(range(runs))
    everything = list(range(CHUNKS))
    moved = (2, 1)
    done = last * CHUNKS
    work = {
        done - 12: [("rows", 0)],
        done - 11: [("rows", 1)],
        done - 9: [((0,), everything[:half], [0, 1], False)],
        done - 8: [(moved, [0, 1], [0, 1], False)],
        done - 7: [((0,), everything[half:], [0, 1], False)],
        done - 6: [(moved, [2, 3], [0, 1], False)],
        done - 5: [("rows", 2)],
        done - 4: [(moved, [4, 5], [0, 1], False)],
        done - 3: [((0,), everything[:half], [2], False)],
        done - 2: [(moved, [0, 1], [2], False)],
        done - 1: [((0,), everything[half:], [2], False)],
        done: [(moved, [2, 3], [2], False)],
        done + 1: [("rows", 3)],
        done + 2: [((0,), everything, [3], True)],
        done + 3: [(moved, [0, half], [3], True)],
        done + 4: [(moved, [1, half + 1], [2, 3], True)],
        done + 5: [(moved, [half - 1, CHUNKS - 1], [2, 3], True)],
    }
    added = set()

    for step in range(steps + 3):
        before = ended.get(step - 2, [])
        if step < CHUNKS:
            first = step * size
            some = tie(start, *[prev for _, prev in kv]) if step == 1 else start
            own[step, 0] = attend(queries, *kv[first // per_kv], some, first, size)
        arrived = []
        if step < len(over_z):
            kind, c, r = over_z[step]
            table = own if kind == "own" else mirror
            value, sums = held(table[c, r - 1], sums, *before)
            table[c, r] = from_behind(value, "dp", 1)
            arrived.append(table[c, r])
        if step < len(over_y):
            c, r = over_y[step]
            value, sums = held(own[c, r], sums, *before)
            mirror[c, r] = over_tensor(value, 2)
            arrived.append(mirror[c, r])
        ended[step] = arrived
        past = step - 2
        swaps = []
        if 0 <= past < steps:
            swaps = [over_y[past]] + [x[1:] for x in over_z[past : past + 1] if x[0] == "mirror"]
        if swaps:
            pair = ([mirror[x] for x in swaps], [own[x] for x in swaps])
            pair, sums = held(pair, sums, *before, *swapped)
            sent = jnp.where(even, *[jnp.concatenate(x, 1) for x in pair])
            sent = over_tensor(sent, 1)
            swapped = [sent]
            sibling.update({x: sent for x in swaps})
            within.update({x: i * width for i, x in enumerate(swaps)})
        for job in work.pop(step, ()):
            if job[0] == "rows":
                ended[step] += rows_for([job[1]])
            else:
                kinds, chosen, some_runs, final = job
                lefts, pieces = rows_for(some_runs), tiles(kinds, chosen, some_runs)
                added.update((k, c, r) for k in kinds for c in chosen for r in some_runs)
                args = (lefts, pieces, width, 3 * slab, scale)
                if final:
                    sums["all"] = gram(sums.get("all"), *args, jnp.float32, sums["half"])
                else:
                    sums["half"] = gram(sums.get("half"), *args, jnp.bfloat16, add=some_runs[0] > 0)
    assert not work and len(added) == 3 * CHUNKS * runs
    return sums["all"]


def per_device_general(queries, keys, values, page_start):
    tok_rows, slab_width = queries.shape
    local_heads = slab_width // HD
    runs = lax.axis_size("dp")
    kv, per_kv = kv_of(keys, values, local_heads)
    run_index = lax.axis_index("dp")
    start = (page_start - run_index * tok_rows).reshape(tok_rows, 1)
    outputs = jnp.concatenate(
        [attend(queries, *kv[h // per_kv], start, h, per_kv) for h in range(0, local_heads, per_kv)], 1
    )
    steps = lax.axis_size("tensor") // 2 + 1
    rows = slab_width // runs
    moving = lax.all_gather(outputs, "dp", axis=0, tiled=True)
    left = lax.dynamic_slice_in_dim(moving, run_index * rows, rows, 1)
    tiles = []
    for offset in range(steps):
        if offset:
            moving = from_behind(moving, "tensor", -1)
        tiles.append(
            lax.dot_general(
                left, moving, (((0,), (0,)), ((), ())), preferred_element_type=jnp.float32
            )
        )
    return jnp.concatenate(tiles, 1) * (2.0 / (tok_rows * runs))


def solution(mesh):
    cores = mesh.shape["tensor"]
    rows = HEADS * HD // cores // mesh.shape["dp"]
    tuned = cores == 4 and rows % HD == 0
    return jax.shard_map(
        per_device if tuned else per_device_general,
        mesh=mesh,
        in_specs=(
            P(("groups", "dp"), "tensor"),
            P(("groups", "dp"), None),
            P(("groups", "dp"), None),
            P(("groups", "dp")),
        ),
        out_specs=P(("groups", "tensor", "dp"), None),
        check_vma=False,
    )
```

```python
import functools

import jax
import jax.numpy as jnp
from jax import lax
from jax.experimental import pallas as pl
from jax.experimental.pallas import tpu as pltpu
from jax.sharding import PartitionSpec as P

HEADS = 96
HD = 128
KV_HEADS = 8
PAGE = 512
TILE = 256
ROWS = 256
STEP = 2
LOG2E = 1.4426950408889634
VMEM_LIMIT = 56 * 1024 * 1024


def shifted(x, axis, by):
    devices = lax.axis_size(axis)
    pairs = [(i, i + by) for i in range(devices) if 0 <= i + by < devices]
    return lax.ppermute(x, axis, pairs)


def from_behind(value, axis, steps):
    count = lax.axis_size(axis)
    pairs = [(source, (source + steps) % count) for source in range(count)]
    return lax.ppermute(value, axis, pairs)


def over_tensor(value, bit):
    count = lax.axis_size("tensor")
    return lax.ppermute(value, "tensor", [(t, t ^ bit) for t in range(count)])


def tie(value, *after):
    return lax.optimization_barrier((value, *after))[0] if after else value


def held(value, sums, *after):
    return lax.optimization_barrier((value, sums, *after))[:2]


def attend_kernel(start_ref, q_ref, kp_ref, ko_ref, vp_ref, vo_ref, out_ref, bias_ref):
    rows = q_ref.shape[0]
    tiles = rows // TILE
    keys_seen = PAGE + TILE

    @pl.when(pl.program_id(0) == 0)
    def _():
        for tile in range(tiles):
            shape = (TILE, keys_seen)
            query = lax.broadcasted_iota(jnp.int32, shape, 0) + tile * TILE
            key = lax.broadcasted_iota(jnp.int32, shape, 1) + (tile * TILE - PAGE)
            first = start_ref[tile * TILE : (tile + 1) * TILE, :]
            visible = (key >= first) & (key <= query)
            bias_ref[tile] = jnp.where(visible, 0.0, -1e30)

    for tile in range(tiles):
        lo = tile * TILE
        key = jnp.concatenate([kp_ref[lo:, :], ko_ref[: lo + TILE, :]], 0)
        value = jnp.concatenate([vp_ref[lo:, :], vo_ref[: lo + TILE, :]], 0)
        value = jnp.concatenate([value, jnp.ones_like(value)], 1)
        for head in range(q_ref.shape[1] // HD):
            columns = slice(head * HD, (head + 1) * HD)
            scores = lax.dot_general(
                q_ref[lo : lo + TILE, columns],
                key,
                (((1,), (1,)), ((), ())),
                preferred_element_type=jnp.float32,
            )
            scores = scores + bias_ref[tile]
            top = jnp.max(scores, axis=-1, keepdims=True)
            expo = jnp.exp2((scores - top) * (LOG2E / HD**0.5)).astype(jnp.bfloat16)
            mixed = jnp.dot(expo, value, preferred_element_type=jnp.float32)
            out_ref[lo : lo + TILE, columns] = (mixed[:, :HD] / mixed[:, HD:]).astype(jnp.bfloat16)


def attend(queries, own_kv, prev_kv, start, first_head, heads):
    rows = queries.shape[0]
    step = heads if first_head == 0 and heads <= 2 * STEP else STEP
    step = step if heads % step == 0 and first_head % step == 0 else 1
    key_spec = pl.BlockSpec((PAGE, HD), lambda h: (0, 0))
    value_spec = pl.BlockSpec((PAGE, HD), lambda h: (0, 1))
    return pl.pallas_call(
        attend_kernel,
        grid=(heads // step,),
        out_shape=jax.ShapeDtypeStruct((rows, heads * HD), jnp.bfloat16),
        in_specs=[
            pl.BlockSpec((rows, 1), lambda h: (0, 0)),
            pl.BlockSpec((rows, step * HD), lambda h: (0, first_head // step + h)),
            key_spec,
            key_spec,
            value_spec,
            value_spec,
        ],
        out_specs=pl.BlockSpec((rows, step * HD), lambda h: (0, h)),
        scratch_shapes=[pltpu.VMEM((rows // TILE, TILE, PAGE + TILE), jnp.float32)],
        compiler_params=pltpu.CompilerParams(vmem_limit_bytes=VMEM_LIMIT),
        cost_estimate=pl.CostEstimate(flops=10**15, bytes_accessed=1, transcendentals=0),
    )(start, queries, prev_kv, own_kv, prev_kv, own_kv)


def rows_kernel(widths, rows, place_ref, *refs):
    chunks = len(widths)
    sources, (out_ref, raw, sem) = refs[:chunks], refs[chunks:]
    offsets = [sum(widths[:c]) for c in range(chunks)]
    for where in range(sum(widths) // rows):

        @pl.when(place_ref[0] == where)
        def _():
            lo, hi = where * rows, (where + 1) * rows
            copies = []
            for c in range(chunks):
                first, last = max(lo, offsets[c]), min(hi, offsets[c] + widths[c])
                if first < last:
                    copies.append(
                        pltpu.make_async_copy(
                            sources[c].at[:, pl.ds(first - offsets[c], last - first)],
                            raw.at[:, pl.ds(first - lo, last - first)],
                            sem.at[len(copies)],
                        )
                    )
            for copy in copies:
                copy.start()
            for copy in copies:
                copy.wait()

    out_ref[...] = raw[...].T


def rows_of(place, pieces, rows):
    depth = pieces[0].shape[0]
    widths = tuple(x.shape[1] for x in pieces)
    return pl.pallas_call(
        functools.partial(rows_kernel, widths, rows),
        out_shape=jax.ShapeDtypeStruct((rows, depth), jnp.bfloat16),
        in_specs=[pl.BlockSpec(memory_space=pltpu.SMEM)]
        + [pl.BlockSpec(memory_space=pltpu.HBM)] * len(pieces),
        scratch_shapes=[
            pltpu.VMEM((depth, rows), jnp.bfloat16),
            pltpu.SemaphoreType.DMA((len(pieces),)),
        ],
        compiler_params=pltpu.CompilerParams(vmem_limit_bytes=VMEM_LIMIT),
        cost_estimate=pl.CostEstimate(flops=10**15, bytes_accessed=1, transcendentals=0),
    )(place, *pieces)


def gram_kernel(runs, tiles, counts, starts, depth, scale, kept, added, in_place, *refs):
    lefts, refs = refs[:runs], refs[runs:]
    data, refs = refs[: len(starts)], list(refs[len(starts) :])
    old_ref = refs.pop(0) if added else None
    if kept and not in_place:
        refs.pop(0)
    out_ref, left, b_buf, o_buf, left_sem, b_sem, o_sem = refs[:7]
    c_buf, c_sem = refs[7:] if added else (None, None)
    slots = b_buf.shape[0]

    def in_copies(i):
        slot = i % slots
        width = tiles[i][1]
        copies = [
            pltpu.make_async_copy(
                data[n].at[:, pl.ds(starts[n], width)],
                b_buf.at[slot, pl.ds(run * depth, depth), pl.ds(0, width)],
                b_sem.at[slot, run],
            )
            for run, n in zip(range(runs - counts[i], runs), range(sum(counts[:i]), sum(counts)))
        ]
        if added:
            copies.append(
                pltpu.make_async_copy(
                    old_ref.at[:, pl.ds(*tiles[i])],
                    c_buf.at[slot, :, pl.ds(0, width)],
                    c_sem.at[slot],
                )
            )
        return copies

    def out_copy(i):
        slot = i % slots
        return pltpu.make_async_copy(
            o_buf.at[slot, :, pl.ds(0, tiles[i][1])],
            out_ref.at[:, pl.ds(*tiles[i])],
            o_sem.at[slot],
        )

    left_copies = [
        pltpu.make_async_copy(
            lefts[run], left.at[:, pl.ds(run * depth, depth)], left_sem.at[run]
        )
        for run in range(runs)
    ]
    for copy in left_copies + in_copies(0):
        copy.start()
    for copy in left_copies:
        copy.wait()
    for i in range(1, min(slots - 1, len(tiles))):
        for copy in in_copies(i):
            copy.start()
    for i, (_, width) in enumerate(tiles):
        slot = i % slots
        if i + slots - 1 < len(tiles):
            for copy in in_copies(i + slots - 1):
                copy.start()
        for copy in in_copies(i):
            copy.wait()
        if i >= slots:
            out_copy(i - slots).wait()

        def block(part, slot=slot, width=width, seen=slice((runs - counts[i]) * depth, None)):
            result = scale * jnp.dot(
                left[part, seen], b_buf[slot, seen, :width], preferred_element_type=jnp.float32
            )
            if added:
                result = result + c_buf[slot, part, :width].astype(jnp.float32)
            o_buf[slot, part, :width] = result.astype(o_buf.dtype)

        if added and not in_place:
            block(slice(None))
        else:
            pl.loop(0, left.shape[0] // ROWS)(lambda n: block(pl.ds(pl.multiple_of(n * ROWS, ROWS), ROWS)))
        out_copy(i).start()
    for i in range(max(0, len(tiles) - slots), len(tiles)):
        out_copy(i).wait()


def gram(out, lefts, tiles, width, columns, scale, kind, old=None, add=False):
    runs = len(lefts)
    rows, depth = lefts[0].shape
    places = [(first, width) for first, _ in tiles]
    data = [x for _, arrays in tiles for x, _ in arrays]
    starts = [x for _, arrays in tiles for _, x in arrays]
    counts = [len(arrays) for _, arrays in tiles]
    kept, added = out is not None, add or old is not None
    any_spec = pl.BlockSpec(memory_space=pltpu.HBM)
    operands = [*lefts, *data] + ([] if old is None else [old]) + ([out] if kept else [])
    slots = min(4, len(tiles))
    scratch = [
        pltpu.VMEM((rows, runs * depth), jnp.bfloat16),
        pltpu.VMEM((slots, runs * depth, width), jnp.bfloat16),
        pltpu.VMEM((slots, rows, width), kind),
        pltpu.SemaphoreType.DMA((runs,)),
        pltpu.SemaphoreType.DMA((slots, runs)),
        pltpu.SemaphoreType.DMA((slots,)),
    ]
    if added:
        scratch += [pltpu.VMEM((slots, rows, width), out.dtype if old is None else old.dtype), pltpu.SemaphoreType.DMA((slots,))]
    total = sum(width for _, width in places)
    return pl.pallas_call(
        functools.partial(gram_kernel, runs, places, counts, starts, depth, scale, kept, added, add),
        out_shape=jax.ShapeDtypeStruct((rows, columns), kind),
        in_specs=[any_spec] * len(operands),
        out_specs=any_spec,
        scratch_shapes=scratch,
        input_output_aliases={len(operands) - 1: 0} if kept else {},
        compiler_params=pltpu.CompilerParams(vmem_limit_bytes=VMEM_LIMIT),
        cost_estimate=pl.CostEstimate(flops=10**15, bytes_accessed=1, transcendentals=0),
    )(*operands)


def kv_of(keys, values, local_heads):
    group = HEADS // KV_HEADS
    kv_count = max(1, local_heads // group)
    kv_first = lax.axis_index("tensor") * local_heads // group
    own, prev = [], []
    for k in range(kv_count):
        parts = [lax.dynamic_slice_in_dim(x, (kv_first + k) * HD, HD, 1) for x in (keys, values)]
        own.append(jnp.concatenate(parts, 1))
        prev.append(shifted(own[k], "dp", 1))
    return list(zip(own, prev)), local_heads // kv_count


CHUNKS = 6


def per_device(queries, keys, values, page_start):
    tok_rows, slab = queries.shape
    local_heads = slab // HD
    runs = lax.axis_size("dp")
    kv, per_kv = kv_of(keys, values, local_heads)
    run_index = lax.axis_index("dp")
    start = (page_start - run_index * tok_rows).reshape(tok_rows, 1)
    place = run_index.reshape(1)
    rows = slab // runs
    scale = 2.0 / (tok_rows * runs)
    even = lax.axis_index("tensor") % 2 == 0

    size = local_heads // CHUNKS
    width = size * HD
    own, mirror, sibling = {}, {}, {}
    within = {}
    half = CHUNKS // 2
    last = runs - 1
    over_z = [("own", c, r) for r in range(1, runs) for c in range(CHUNKS)]
    over_z += [("mirror", c, last) for c in range(half, CHUNKS)]
    over_y = [(c, r) for r in range(last) for c in range(CHUNKS)]
    over_y += [(c, last) for c in range(half)]

    left = {}
    sums = {}
    steps = max(len(over_z), len(over_y))
    ended = {}
    swapped = []
    def tiles(kinds, chosen, some_runs):
        tables = (own, sibling, mirror)
        return [
            (
                k * slab + c * width,
                [
                    (tables[k][c, r], within[c, r] if k == 1 else 0)
                    for r in some_runs
                    if (k, c, r) not in added
                ],
            )
            for c in chosen
            for k in kinds
        ]

    def rows_for(some_runs):
        for r in some_runs:
            if r not in left:
                left[r] = rows_of(place, [own[c, r] for c in range(CHUNKS)], rows)
        return [left[r] for r in some_runs]

    every = list(range(runs))
    everything = list(range(CHUNKS))
    moved = (2, 1)
    done = last * CHUNKS
    work = {
        done - 12: [("rows", 0)],
        done - 11: [("rows", 1)],
        done - 9: [((0,), everything[:half], [0, 1], False)],
        done - 8: [(moved, [0, 1], [0, 1], False)],
        done - 7: [((0,), everything[half:], [0, 1], False)],
        done - 6: [(moved, [2, 3], [0, 1], False)],
        done - 5: [("rows", 2)],
        done - 4: [(moved, [4, 5], [0, 1], False)],
        done - 3: [((0,), everything[:half], [2], False)],
        done - 2: [(moved, [0, 1], [2], False)],
        done - 1: [((0,), everything[half:], [2], False)],
        done: [(moved, [2, 3], [2], False)],
        done + 1: [("rows", 3)],
        done + 2: [((0,), everything, [3], True)],
        done + 3: [(moved, [0, half], [3], True)],
        done + 4: [(moved, [1, half + 1], [2, 3], True)],
        done + 5: [(moved, [half - 1, CHUNKS - 1], [2, 3], True)],
    }
    added = set()

    for step in range(steps + 3):
        before = ended.get(step - 2, [])
        if step < CHUNKS:
            first = step * size
            own[step, 0] = attend(queries, *kv[first // per_kv], start, first, size)
        arrived = []
        if step < len(over_z):
            kind, c, r = over_z[step]
            table = own if kind == "own" else mirror
            value, sums = held(table[c, r - 1], sums, *before)
            table[c, r] = from_behind(value, "dp", 1)
            arrived.append(table[c, r])
        if step < len(over_y):
            c, r = over_y[step]
            value, sums = held(own[c, r], sums, *before)
            mirror[c, r] = over_tensor(value, 2)
            arrived.append(mirror[c, r])
        ended[step] = arrived
        past = step - 2
        swaps = []
        if 0 <= past < steps:
            swaps = [over_y[past]] + [x[1:] for x in over_z[past : past + 1] if x[0] == "mirror"]
        if swaps:
            pair = ([mirror[x] for x in swaps], [own[x] for x in swaps])
            pair, sums = held(pair, sums, *before, *swapped)
            sent = jnp.where(even, *[jnp.concatenate(x, 1) for x in pair])
            sent = over_tensor(sent, 1)
            swapped = [sent]
            sibling.update({x: sent for x in swaps})
            within.update({x: i * width for i, x in enumerate(swaps)})
        for job in work.pop(step, ()):
            if job[0] == "rows":
                ended[step] += rows_for([job[1]])
            else:
                kinds, chosen, some_runs, final = job
                lefts, pieces = rows_for(some_runs), tiles(kinds, chosen, some_runs)
                added.update((k, c, r) for k in kinds for c in chosen for r in some_runs)
                args = (lefts, pieces, width, 3 * slab, scale)
                if final:
                    sums["all"] = gram(sums.get("all"), *args, jnp.float32, sums["half"])
                else:
                    sums["half"] = gram(sums.get("half"), *args, jnp.bfloat16, add=some_runs[0] > 0)
    assert not work and len(added) == 3 * CHUNKS * runs
    return sums["all"]


def per_device_general(queries, keys, values, page_start):
    tok_rows, slab_width = queries.shape
    local_heads = slab_width // HD
    runs = lax.axis_size("dp")
    kv, per_kv = kv_of(keys, values, local_heads)
    run_index = lax.axis_index("dp")
    start = (page_start - run_index * tok_rows).reshape(tok_rows, 1)
    outputs = jnp.concatenate(
        [attend(queries, *kv[h // per_kv], start, h, per_kv) for h in range(0, local_heads, per_kv)], 1
    )
    steps = lax.axis_size("tensor") // 2 + 1
    rows = slab_width // runs
    moving = lax.all_gather(outputs, "dp", axis=0, tiled=True)
    left = lax.dynamic_slice_in_dim(moving, run_index * rows, rows, 1)
    tiles = []
    for offset in range(steps):
        if offset:
            moving = from_behind(moving, "tensor", -1)
        tiles.append(
            lax.dot_general(
                left, moving, (((0,), (0,)), ((), ())), preferred_element_type=jnp.float32
            )
        )
    return jnp.concatenate(tiles, 1) * (2.0 / (tok_rows * runs))


def solution(mesh):
    cores = mesh.shape["tensor"]
    rows = HEADS * HD // cores // mesh.shape["dp"]
    tuned = cores == 4 and rows % HD == 0
    return jax.shard_map(
        per_device if tuned else per_device_general,
        mesh=mesh,
        in_specs=(
            P(("groups", "dp"), "tensor"),
            P(("groups", "dp"), None),
            P(("groups", "dp"), None),
            P(("groups", "dp")),
        ),
        out_specs=P(("groups", "tensor", "dp"), None),
        check_vma=False,
    )
```
